128 devices in a mesh: tm: 16 (over x, y_hi, core), head: 8 (over y_lo, z).
Axes of the slice: x: 4, y: 4 (y_hi: 2, y_lo: 2; y = y_hi * 2 + y_lo), z: 4, core: 2. Of those that a mesh axis runs over, the one named last changes fastest.
Arguments:
- q_in: bfloat16 [16, 1536, 5120], P('tm', 'head'), may hold values from -256 to 256
- k_in: bfloat16 [16, 1536, 5120], P('tm', 'head'), may hold values from -256 to 256
- v_in: bfloat16 [16, 1536, 5120], P('tm', 'head'), may hold values from -6 to 6
- q_gain: float32 [5120], replicated, may hold values from 0.5 to 2
- k_gain: float32 [5120], replicated, may hold values from 0.5 to 2
- keep_one: int32 [16, 2, 6], replicated, may hold values from 0 to 11, as said below
- keep_two: int32 [16, 2, 3], replicated, may hold values from 0 to 11, as said below
- keep_four: int32 [16, 2, 1], replicated, may hold values from 0 to 11, as said below
- keep_eight: int32 [16, 2, 1], replicated, may hold values from 0 to 11, as said below
Outputs:
- attended: bfloat16 [16, 1536, 5120], P('tm', 'head')
The draws below stay inside these ranges and needn't reach their ends.
Inputs may be any that keep to these rules, and one draw needn't show every extreme that they name: `keep_one`: each row lists distinct block numbers of a frame in increasing order. `keep_two`: each row lists distinct block numbers of a frame in increasing order. `keep_four`: each row lists distinct block numbers of a frame in increasing order. `keep_eight`: each row lists distinct block numbers of a frame in increasing order.
All inputs are finite; a program needn't handle non-finite values.
Results may differ from the reference program's by a relative error of at most 0.0025.
The reference program's roundings to bfloat16 on the way (of `q_norm`, `k_norm` and `weights`) count: a program that leaves them out, or rounds other values in their place, can miss the bound.
Values may be sent and summed in bfloat16 or wider, within the bound.
A program may use at most 192 MiB of HBM per device.

```python
import math
import jax
import jax.numpy as jnp
from jax import lax

HEADS = 40
HD = 128
D = 5120
S = 1536
BLK = 128
NB = 12
KB1 = 6
KB2 = 3
KB4 = 1
KB8 = 1
FRAMES = 16


def draw_k_in(key, part):
    key = jax.random.fold_in(key, 11)
    base = jax.random.normal(key, (FRAMES, S, D), dtype=jnp.float32)
    return base.astype(jnp.bfloat16)


def draw_q_in(key, part):
    key = jax.random.fold_in(key, 13)
    base = jax.random.normal(key, (FRAMES, S, D), dtype=jnp.float32)
    return base.astype(jnp.bfloat16)


def keep_rows(key, kept_count):
    scores = jax.random.randint(key, (FRAMES, 2, NB), 0, 1048576) * NB + jnp.arange(NB)
    scores = scores.at[0, 0, NB - 1].set(-1).at[0, 1, 0].set(-1)
    order = jnp.argsort(scores, axis=-1)
    return jnp.sort(order[..., :kept_count], axis=-1).astype(jnp.int32)


def draw_keep_one(key, part):
    key = jax.random.fold_in(key, 31)
    return keep_rows(key, KB1)


def draw_keep_two(key, part):
    key = jax.random.fold_in(key, 32)
    return keep_rows(key, KB2)


def draw_keep_four(key, part):
    key = jax.random.fold_in(key, 33)
    return keep_rows(key, KB4)


def draw_keep_eight(key, part):
    key = jax.random.fold_in(key, 34)
    return keep_rows(key, KB8)


def levels(key, extent, shards, least, top_value):
    level = 1.0
    for axis_at, blocks in shards:
        draws = jax.random.uniform(jax.random.fold_in(jax.random.fold_in(key, 6), axis_at), (blocks,), jnp.float32, least / len(shards), top_value / len(shards))
        level = level * jnp.repeat(jnp.exp(draws), extent[axis_at] // blocks).reshape((-1,) + (1,) * (len(extent) - 1 - axis_at))
    return level


def normal_values(rng, dims, scale, reach, cuts=(), held_as=jnp.bfloat16):
    values = jax.random.normal(rng, dims, jnp.float32) * scale
    if len(cuts) > 0:
        values = levels(rng, dims, cuts, -0.22, 0.18) * values
    return jnp.clip(values, min=-reach, max=reach).astype(held_as)


def setup_inputs(seed: int = 0) -> dict:
    key_list = jax.random.split(jax.random.key(seed), 10)
    q_in = draw_q_in(jax.random.fold_in(key_list[9], 71), 0)
    k_in = draw_k_in(jax.random.fold_in(key_list[9], 71), 0)
    v_in = normal_values(key_list[2], (FRAMES, S, D), 1.0, 6.0, ((0, 16), (1, 8)))
    q_gain = jnp.clip(jnp.exp(jax.random.uniform(key_list[3], (D,), jnp.float32, math.log(0.5), math.log(2.0))), 0.5, 2.0)
    k_gain = jnp.clip(jnp.exp(jax.random.uniform(key_list[4], (D,), jnp.float32, math.log(0.5), math.log(2.0))), 0.5, 2.0)
    keep_one = draw_keep_one(jax.random.fold_in(key_list[9], 71), 0)
    keep_two = draw_keep_two(jax.random.fold_in(key_list[9], 71), 0)
    keep_four = draw_keep_four(jax.random.fold_in(key_list[9], 71), 0)
    keep_eight = draw_keep_eight(jax.random.fold_in(key_list[9], 71), 0)
    return dict(q_in=q_in, k_in=k_in, v_in=v_in, q_gain=q_gain, k_gain=k_gain, keep_one=keep_one, keep_two=keep_two, keep_four=keep_four, keep_eight=keep_eight)


EPSILON = 1e-06
NEGATIVE = -1e+30

def normalize(values, gain):
    wide = values.astype(jnp.float32)
    meansq = lax.optimization_barrier(jnp.mean(wide * wide, axis=-1, keepdims=True))
    return (wide * lax.rsqrt(meansq + EPSILON) * gain).astype(jnp.bfloat16)

def reference(q_in, k_in, v_in, q_gain, k_gain, keep_one, keep_two, keep_four, keep_eight):
    q_norm = normalize(q_in, q_gain)
    k_norm = normalize(k_in, k_gain)
    frames = q_in.shape[0]
    blocks = S // BLK
    scale = 1.0 / math.sqrt(HD)
    keeps = ((1, keep_one), (2, keep_two), (4, keep_four), (8, keep_eight))

    def per_frame(frame):
        key_parts = [k_norm[frame]]
        value_parts = [v_in[frame]]
        usable_parts = [jnp.ones((S,), dtype=bool)]
        for distance, keep in keeps:
            kept_count = keep.shape[2]
            for direction, other in ((0, frame - distance), (1, frame + distance)):
                clipped = jnp.clip(other, 0, frames - 1).astype(jnp.int32)
                chosen = keep[frame, direction]
                key_blocks = k_norm[clipped].reshape(blocks, BLK, D)[chosen]
                value_blocks = v_in[clipped].reshape(blocks, BLK, D)[chosen]
                key_parts.append(key_blocks.reshape(kept_count * BLK, D))
                value_parts.append(value_blocks.reshape(kept_count * BLK, D))
                inside = jnp.logical_and(other >= 0, other < frames)
                usable_parts.append(jnp.full((kept_count * BLK,), inside))
        keys_all = jnp.concatenate(key_parts, axis=0)
        values_all = jnp.concatenate(value_parts, axis=0)
        usable = jnp.concatenate(usable_parts, axis=0)
        queries = q_norm[frame].reshape(S, HEADS, HD).transpose(1, 0, 2)
        key_heads = keys_all.reshape(-1, HEADS, HD).transpose(1, 0, 2)
        value_heads = values_all.reshape(-1, HEADS, HD).transpose(1, 0, 2)

        def per_head(operands):
            query_rows, key_rows, value_rows = operands
            scores = jnp.dot(query_rows, key_rows.T, preferred_element_type=jnp.float32) * scale
            scores = jnp.where(usable[None, :], scores, NEGATIVE)
            top = lax.optimization_barrier(jnp.max(scores, axis=-1, keepdims=True))
            expo = jnp.exp(scores - top)
            totals = lax.optimization_barrier(jnp.sum(expo, axis=-1, keepdims=True))
            weights = expo.astype(jnp.bfloat16)
            summed = jnp.dot(weights, value_rows, preferred_element_type=jnp.float32)
            return (summed / totals).astype(jnp.bfloat16)
        result = lax.map(per_head, (queries, key_heads, value_heads))
        return result.transpose(1, 0, 2).reshape(S, D)
    return lax.map(per_frame, jnp.arange(frames).astype(jnp.int32))
```

```python
import functools
import math

import jax
import jax.numpy as jnp
from jax import lax
from jax.experimental import pallas as pl
from jax.experimental.pallas import tpu as pltpu
from jax.sharding import PartitionSpec as P

MESH = pl.DeviceIdType.MESH
HEADS = 40
HD = 128
BLK = 128
EPSILON = 1e-06
NEGATIVE = -1e30
LOG2E = math.log2(math.e)

FRAMES = 16
MEMBERS = 8
PER = HEADS // MEMBERS
TOKENS = 192
S = TOKENS * MEMBERS
NB = S // BLK
WIDTH = HEADS * HD
SEGMENTS = ((1, 0, 6, 0), (1, 1, 6, 6), (2, 0, 3, 12), (2, 1, 3, 15), (4, 0, 1, 18), (4, 1, 1, 19), (8, 0, 1, 20), (8, 1, 1, 20))
KEPT = 21
KEYS = (NB + KEPT) * BLK
CHUNK = 11
TQ = 512
NORM_ROWS = 32


def nt_dot(a, b):
    return lax.dot_general(a, b, (((1,), (1,)), ((), ())), preferred_element_type=jnp.float32)


def reaches(frame, distance, direction):
    room = frame if direction == 0 else FRAMES - 1 - frame
    return jnp.minimum(room // distance, 1)


def first_block(frame, segment):
    at = NB
    for distance, direction, count, _ in SEGMENTS[:segment]:
        if distance < 8:
            at = at + count * reaches(frame, distance, direction)
    return at


def kernel(
    q_hbm, k_hbm, v_hbm, q_gain, k_gain, keep_one, keep_two, keep_four, keep_eight,
    out_hbm,
    q_in, k_in, v_in, q_norm, k_norm, queries, pairs, stage, kept, heads_out,
    load_sem, own_sem, a2a_send, a2a_recv, kept_send, kept_recv, out_send, out_recv,
):
    frame = lax.axis_index("tm")
    member = lax.axis_index("head")
    keeps = {1: keep_one, 2: keep_two, 4: keep_four, 8: keep_eight}

    def y_hi(f):
        return (f // 2) % 2

    def flip(m, bits):
        total = 0
        for b in (1, 2, 4):
            x = (m // b) % 2 + (bits // b) % 2
            total = total + b * (x % 2)
        return total

    def group_of(f, m):
        return flip(m, 4 * y_hi(f))

    mine = group_of(frame, member)
    partners = [flip(member, j) for j in range(MEMBERS)]
    their_groups = [group_of(frame, p) for p in partners]

    def rows_of(m):
        return pl.ds(pl.multiple_of(m * TOKENS, 64), TOKENS)

    loads = [
        pltpu.make_async_copy(v_hbm.at[0], v_in, load_sem.at[0]),
        pltpu.make_async_copy(k_hbm.at[0], k_in, load_sem.at[1]),
        pltpu.make_async_copy(q_hbm.at[0], q_in, load_sem.at[2]),
    ]
    for load in loads:
        load.start()

    first_idle = (NB + 11) * BLK
    for h in range(PER):
        for t in range(2):
            pairs[h, t, first_idle:, :] = jnp.zeros((KEYS - first_idle, HD), jnp.bfloat16)

    def kept_links(f):
        links = []
        for distance, direction, count, at in SEGMENTS:
            sign = 1 if direction == 0 else -1
            to = f + sign * distance
            source = f - sign * distance
            sends = jnp.logical_and(to >= 0, to < FRAMES)
            takes = jnp.logical_and(source >= 0, source < FRAMES)
            to_in = jnp.clip(to, 0, FRAMES - 1)
            links.append((sends, takes, to_in, flip(member, 4 * ((y_hi(to_in) + y_hi(f)) % 2))))
        return links

    links = kept_links(frame)

    barrier = pltpu.get_barrier_semaphore()
    for j in range(1, MEMBERS):
        pl.semaphore_signal(barrier, inc=1, device_id=(frame, partners[j]), device_id_type=MESH)
    expected = MEMBERS - 1
    for sends, takes, to, peer in links:
        @pl.when(sends)
        def _():
            pl.semaphore_signal(barrier, inc=1, device_id=(to, peer), device_id_type=MESH)

    for distance, direction, _, _ in SEGMENTS:
        expected = expected + reaches(frame, distance, 1 - direction)
    pl.semaphore_wait(barrier, expected)

    def lanes_of(head):
        return pl.ds(pl.multiple_of(head * HD, HD), HD)

    def exchange(t, h, j):
        head = their_groups[j] * PER + h
        if t == 0:
            source, target = v_in.at[:, lanes_of(head)], pairs.at[h, 1, rows_of(member)]
        elif t == 1:
            source, target = k_norm.at[head], pairs.at[h, 0, rows_of(member)]
        else:
            source, target = q_norm.at[head], queries.at[h, rows_of(member)]
        if j == 0:
            return pltpu.make_async_copy(source, target, own_sem.at[t, h])
        return pltpu.make_async_remote_copy(
            source, target, a2a_send.at[t, h, j - 1], a2a_recv.at[t, h, j - 1],
            device_id=(frame, partners[j]), device_id_type=MESH,
        )

    def arrival(t, h, j):
        rows = rows_of(partners[j])
        target = (pairs.at[h, 1, rows], pairs.at[h, 0, rows], queries.at[h, rows])[t]
        return pltpu.make_async_copy(target, target, a2a_recv.at[t, h, j - 1])

    def start_exchange(t, h):
        for j in range(1, MEMBERS):
            exchange(t, h, j).start()
        exchange(t, h, 0).start()

    def wait_exchange(t, h):
        exchange(t, h, 0).wait()
        for j in range(1, MEMBERS):
            arrival(t, h, j).wait()

    def normalise(source, gain, target):
        scale = gain[...]

        def some_rows(i, carry):
            rows = pl.ds(pl.multiple_of(i * NORM_ROWS, NORM_ROWS), NORM_ROWS)
            wide = source[rows, :].astype(jnp.float32)
            meansq = jnp.mean(wide * wide, axis=-1, keepdims=True)
            normed = (wide * lax.rsqrt(meansq + EPSILON) * scale).astype(jnp.bfloat16)
            for head in range(HEADS):
                target[head, rows, :] = normed[:, head * HD : (head + 1) * HD]
            return carry

        lax.fori_loop(0, TOKENS // NORM_ROWS, some_rows, 0)

    def kept_copy(segment, h):
        distance, direction, count, at = SEGMENTS[segment]
        _, _, to, peer = links[segment]
        start = pl.multiple_of(first_block(to, segment) * BLK, BLK)
        return pltpu.make_async_remote_copy(
            kept.at[h, :, pl.ds(at * BLK, count * BLK)], pairs.at[h, :, pl.ds(start, count * BLK)],
            kept_send.at[h, segment], kept_recv.at[h, segment],
            device_id=(to, peer), device_id_type=MESH,
        )

    def kept_arrival(segment, h):
        count = SEGMENTS[segment][2]
        start = pl.multiple_of(first_block(frame, segment) * BLK, BLK)
        target = pairs.at[h, :, pl.ds(start, count * BLK)]
        return pltpu.make_async_copy(target, target, kept_recv.at[h, segment])

    def send_kept(h):
        for t in range(2):
            stage[t] = pairs[h, t, :S, :].reshape(NB, BLK, HD)
        for segment, (distance, direction, count, at) in enumerate(SEGMENTS):
            sends, _, to, _ = links[segment]

            @pl.when(sends)
            def _():
                for i in range(count):
                    block = keeps[distance][to, direction, i]
                    for t in range(2):
                        kept[h, t, (at + i) * BLK : (at + i + 1) * BLK, :] = stage[t, block]
                kept_copy(segment, h).start()

    def wait_kept(h):
        for segment in range(len(SEGMENTS)):
            @pl.when(links[segment][1])
            def _():
                kept_arrival(segment, h).wait()

    usable_blocks = first_block(frame, len(SEGMENTS)) + 1

    def attend(h):
        scale = LOG2E / math.sqrt(HD)

        def some_queries(i, carry):
            rows = pl.ds(pl.multiple_of(i * TQ, TQ), TQ)
            q = queries[h, rows, :]
            top = jnp.full((TQ, HD), NEGATIVE, jnp.float32)
            total = jnp.zeros((TQ, HD), jnp.float32)
            summed = jnp.zeros((TQ, HD), jnp.float32)
            for chunk in range((NB + KEPT) // CHUNK):
                keys = slice(chunk * CHUNK * BLK, (chunk + 1) * CHUNK * BLK)
                scores = nt_dot(q, pairs[h, 0, keys, :])
                parts = []
                for b in range(CHUNK):
                    part = scores[:, b * BLK : (b + 1) * BLK]
                    if chunk * CHUNK + b >= NB + 11:
                        part = part + jnp.where(chunk * CHUNK + b < usable_blocks, 0.0, NEGATIVE)
                    parts.append(part)
                peak = functools.reduce(jnp.maximum, parts)
                above = jnp.maximum(top, jnp.max(peak, axis=1, keepdims=True) * scale)
                fade = jnp.exp2(top - above)
                weights = jnp.concatenate(
                    [jnp.exp2(part * scale - above).astype(jnp.bfloat16) for part in parts], axis=1
                )
                wide = jnp.concatenate(
                    [pairs[h, 1, keys, :], jnp.ones((CHUNK * BLK, HD), jnp.bfloat16)], axis=1
                )
                product = jnp.dot(weights, wide, preferred_element_type=jnp.float32)
                summed = summed * fade + product[:, :HD]
                total = total * fade + product[:, HD:]
                top = above
            heads_out[h, rows, :] = (summed / total).astype(jnp.bfloat16)
            return carry

        lax.fori_loop(0, S // TQ, some_queries, 0)

    def give_back(h, j):
        lanes = lanes_of(mine * PER + h)
        if j == 0:
            return pltpu.make_async_copy(
                heads_out.at[h, rows_of(member)], out_hbm.at[0, :, lanes], own_sem.at[3, h]
            )
        return pltpu.make_async_remote_copy(
            heads_out.at[h, rows_of(partners[j])], out_hbm.at[0, :, lanes],
            out_send.at[h, j - 1], out_recv.at[h, j - 1],
            device_id=(frame, partners[j]), device_id_type=MESH,
        )

    def returned(h, j):
        target = out_hbm.at[0, :, lanes_of(their_groups[j] * PER + h)]
        return pltpu.make_async_copy(target, target, out_recv.at[h, j - 1])

    loads[0].wait()
    start_exchange(0, 0)
    loads[1].wait()
    normalise(k_in, k_gain, k_norm)
    start_exchange(1, 0)
    loads[2].wait()
    normalise(q_in, q_gain, q_norm)
    start_exchange(2, 0)
    for t in range(3):
        start_exchange(t, 1)
    wait_exchange(0, 0)
    wait_exchange(1, 0)
    send_kept(0)

    def step(h, carry):
        @pl.when(h + 2 < PER)
        def _():
            for t in range(3):
                start_exchange(t, h + 2)

        @pl.when(h + 1 < PER)
        def _():
            wait_exchange(0, h + 1)
            wait_exchange(1, h + 1)
            send_kept(h + 1)

        wait_exchange(2, h)
        wait_kept(h)
        attend(h)
        for j in range(MEMBERS):
            give_back(h, j).start()
        return carry

    lax.fori_loop(0, PER, step, 0)

    def finish(h, carry):
        for j in range(1, MEMBERS):
            for t in range(3):
                exchange(t, h, j).wait_send()
            give_back(h, j).wait_send()
            returned(h, j).wait()
        give_back(h, 0).wait()
        for segment in range(len(SEGMENTS)):
            @pl.when(links[segment][0])
            def _():
                kept_copy(segment, h).wait_send()
        return carry

    lax.fori_loop(0, PER, finish, 0)


def on_device(q_in, k_in, v_in, q_gain, k_gain, keep_one, keep_two, keep_four, keep_eight):
    hbm = pl.BlockSpec(memory_space=pl.ANY)
    vmem = pl.BlockSpec(memory_space=pltpu.VMEM)
    smem = pl.BlockSpec(memory_space=pltpu.SMEM)
    bf16 = jnp.bfloat16
    dma = pltpu.SemaphoreType.DMA
    return pl.pallas_call(
        kernel,
        out_shape=jax.ShapeDtypeStruct((1, TOKENS, WIDTH), bf16),
        in_specs=[hbm, hbm, hbm, vmem, vmem, smem, smem, smem, smem],
        out_specs=hbm,
        scratch_shapes=[
            pltpu.VMEM((TOKENS, WIDTH), bf16),
            pltpu.VMEM((TOKENS, WIDTH), bf16),
            pltpu.VMEM((TOKENS, WIDTH), bf16),
            pltpu.VMEM((HEADS, TOKENS, HD), bf16),
            pltpu.VMEM((HEADS, TOKENS, HD), bf16),
            pltpu.VMEM((PER, S, HD), bf16),
            pltpu.VMEM((PER, 2, KEYS, HD), bf16),
            pltpu.VMEM((2, NB, BLK, HD), bf16),
            pltpu.VMEM((PER, 2, (KEPT + 1) * BLK, HD), bf16),
            pltpu.VMEM((PER, S, HD), bf16),
            dma((3,)),
            dma((4, PER)),
            dma((3, PER, MEMBERS - 1)),
            dma((3, PER, MEMBERS - 1)),
            dma((PER, len(SEGMENTS))),
            dma((PER, len(SEGMENTS))),
            dma((PER, MEMBERS - 1)),
            dma((PER, MEMBERS - 1)),
        ],
        compiler_params=pltpu.CompilerParams(
            collective_id=0, has_side_effects=True, vmem_limit_bytes=60 * 2**20
        ),
        cost_estimate=pl.CostEstimate(
            flops=4 * S * KEYS * PER * HD, bytes_accessed=8 * TOKENS * WIDTH, transcendentals=S * KEYS * PER
        ),
        name="attend",
    )(
        q_in, k_in, v_in, q_gain.reshape(1, WIDTH), k_gain.reshape(1, WIDTH),
        keep_one, keep_two, keep_four, keep_eight,
    )


def solution(mesh):
    return jax.shard_map(
        on_device,
        mesh=mesh,
        in_specs=(P("tm", "head", None),) * 3 + (P(),) * 6,
        out_specs=P("tm", "head", None),
        check_vma=False,
    )
```

```python
import functools
import math

import jax
import jax.numpy as jnp
from jax import lax
from jax.experimental import pallas as pl
from jax.experimental.pallas import tpu as pltpu
from jax.sharding import PartitionSpec as P

MESH = pl.DeviceIdType.MESH
HEADS = 40
HD = 128
BLK = 128
EPSILON = 1e-06
NEGATIVE = -1e30
LOG2E = math.log2(math.e)

FRAMES = 16
MEMBERS = 8
PER = HEADS // MEMBERS
TOKENS = 192
S = TOKENS * MEMBERS
NB = S // BLK
WIDTH = HEADS * HD
SEGMENTS = ((1, 0, 6, 0), (1, 1, 6, 6), (2, 0, 3, 12), (2, 1, 3, 15), (4, 0, 1, 18), (4, 1, 1, 19), (8, 0, 1, 20), (8, 1, 1, 20))
KEPT = 21
UNITS = 5
ORDER = (0, 1, 2, 3, 4, 5, 6, 7)
KEYS = (NB + KEPT) * BLK
TQ = 512
TILES = S // TQ
CHUNKS = ((NB, NB + 11), (NB + 11, NB + KEPT))
SCALE = LOG2E / math.sqrt(HD)
NORM_ROWS = 32


def nt_dot(a, b):
    return lax.dot_general(a, b, (((1,), (1,)), ((), ())), preferred_element_type=jnp.float32)


def reaches(frame, distance, direction):
    room = frame if direction == 0 else FRAMES - 1 - frame
    return jnp.minimum(room // distance, 1)


def first_block(frame, segment):
    at = NB
    for distance, direction, count, _ in SEGMENTS[:segment]:
        if distance < 8:
            at = at + count * reaches(frame, distance, direction)
    return at


def kernel(
    q_hbm, k_hbm, v_hbm, q_gain, k_gain, keep_one, keep_two, keep_four, keep_eight,
    out_hbm,
    q_in, k_in, v_in, q_norm, k_norm, queries, pairs, stage, kept, heads_out, running,
    load_sem, own_sem, a2a_send, a2a_recv, kept_send, kept_recv, out_send, out_recv,
):
    frame = lax.axis_index("tm")
    member = lax.axis_index("head")
    plane, role, core = frame // 4, (frame // 2) % 2, frame % 2
    keeps = {1: keep_one, 2: keep_two, 4: keep_four, 8: keep_eight}

    def flip(m, bits):
        total = 0
        for b in (1, 2, 4):
            x = (m // b) % 2 + (bits // b) % 2
            total = total + b * (x % 2)
        return total

    roles = [(role + other) % 2 for other in range(2)]
    members = [flip(member, j) for j in range(MEMBERS)]

    def place(i):
        return 4 * plane + 2 * roles[i // MEMBERS] + core, members[i % MEMBERS]

    def head_at(s, i):
        its_role = roles[i // MEMBERS]
        group = flip(members[i % MEMBERS], 4 * its_role)
        return group * PER + (2 * its_role + s if s < 2 else 4)

    def unit_of(s, i):
        return 2 * s + i // MEMBERS if s < 2 else 4

    def partners_of(unit):
        first = MEMBERS * (unit % 2)
        return range(first, first + MEMBERS)

    def frame_of(unit):
        return 4 * plane + 2 * ((role + unit % 2) % 2) + core

    def rows_of(m):
        return pl.ds(pl.multiple_of(m * TOKENS, 64), TOKENS)

    def lanes_of(head):
        return pl.ds(pl.multiple_of(head * HD, HD), HD)

    loads = [
        pltpu.make_async_copy(v_hbm.at[0], v_in, load_sem.at[0]),
        pltpu.make_async_copy(k_hbm.at[0], k_in, load_sem.at[1]),
        pltpu.make_async_copy(q_hbm.at[0], q_in, load_sem.at[2]),
    ]
    for load in loads:
        load.start()

    barrier = pltpu.get_barrier_semaphore()

    def greet(device):
        pl.semaphore_signal(barrier, inc=1, device_id=device, device_id_type=MESH)

    first_idle = (NB + 11) * BLK
    for u in range(UNITS):
        for t in range(2):
            pairs[u, t, first_idle:, :] = jnp.zeros((KEYS - first_idle, HD), jnp.bfloat16)

    for i in range(1, 2 * MEMBERS):
        greet(place(i))
    greet((frame + 1 - 2 * core, member))
    expected = 2 * MEMBERS
    near = jnp.minimum(3 - plane, 1), jnp.minimum(plane, 1)
    far = (3 - plane) // 2, plane // 2
    far = jnp.minimum(far[0], 1), jnp.minimum(far[1], 1)
    across = core * near[0] + (1 - core) * near[1]
    side = 2 * core - 1
    meets = [
        (near[0], frame + 4), (near[1], frame - 4), (far[0], frame + 8), (far[1], frame - 8),
        (across, frame + 4 * side - side),
    ]
    for there, to in meets:
        expected = expected + there

        @pl.when(there > 0)
        def _():
            greet((to, member))

    def target_frame(f, segment):
        distance, direction, _, _ = SEGMENTS[segment]
        return f + distance if direction == 0 else f - distance

    def clipped(f):
        return jnp.clip(f, 0, FRAMES - 1)

    def role_of(f):
        return (f // 2) % 2

    def single_place(to):
        return to, flip(member, 4 * ((role_of(to) + role) % 2))

    for segment, (distance, direction, _, _) in enumerate(SEGMENTS):
        to = target_frame(frame, segment)
        there = reaches(frame, distance, 1 - direction)
        expected = expected + there

        @pl.when(there > 0)
        def _():
            greet(single_place(clipped(to)))

    pl.semaphore_wait(barrier, expected)

    def exchange(t, s, i):
        head, unit = head_at(s, i), unit_of(s, i)
        if t == 0:
            source, target = v_in.at[:, lanes_of(head)], pairs.at[unit, 1, rows_of(member)]
        elif t == 1:
            source, target = k_norm.at[head], pairs.at[unit, 0, rows_of(member)]
        else:
            source, target = q_norm.at[head], queries.at[unit, rows_of(member)]
        if i == 0:
            return pltpu.make_async_copy(source, target, own_sem.at[t, s])
        return pltpu.make_async_remote_copy(
            source, target, a2a_send.at[t, s, i], a2a_recv.at[t, s, i],
            device_id=place(i), device_id_type=MESH,
        )

    def start_exchange(t, unit):
        for i in partners_of(unit):
            exchange(t, unit // 2, i).start()

    def wait_exchange(t, unit):
        s = unit // 2
        for i in partners_of(unit):
            if i == 0:
                exchange(t, s, 0).wait()
                continue
            rows = rows_of(members[i % MEMBERS])
            target = (pairs.at[unit, 1, rows], pairs.at[unit, 0, rows], queries.at[unit, rows])[t]
            pltpu.make_async_copy(target, target, a2a_recv.at[t, s, i]).wait()

    def normalise(source, gain, target):
        scale = gain[...]

        def some_rows(i, carry):
            rows = pl.ds(pl.multiple_of(i * NORM_ROWS, NORM_ROWS), NORM_ROWS)
            wide = source[rows, :].astype(jnp.float32)
            meansq = jnp.mean(wide * wide, axis=-1, keepdims=True)
            normed = (wide * lax.rsqrt(meansq + EPSILON) * scale).astype(jnp.bfloat16)
            for head in range(HEADS):
                target[head, rows, :] = normed[:, head * HD : (head + 1) * HD]
            return carry

        lax.fori_loop(0, TOKENS // NORM_ROWS, some_rows, 0)

    def inside(f, segment, unit):
        distance, direction, _, _ = SEGMENTS[segment]
        there = reaches(f, distance, 1 - direction)
        if distance != 2 or unit == 4:
            return there, None
        here = 1 - role_of(f) if direction == 0 else role_of(f)
        return there * (1 - here), here

    def kept_copy(segment, unit, piece=None):
        _, _, count, at = SEGMENTS[segment]
        to = clipped(target_frame(frame_of(unit), segment))
        start = pl.multiple_of(first_block(to, segment) * BLK, BLK)
        if unit == 4:
            device, its_unit = single_place(to), 4
        else:
            device = (4 * (to // 4) + 2 * role + to % 2, member)
            its_unit = 2 * (unit // 2) + (role_of(to) + role) % 2
        source, target = kept.at[unit, :, pl.ds(at * BLK, count * BLK)], pairs.at[its_unit, :, pl.ds(start, count * BLK)]
        if piece is not None:
            i, t = piece
            source = kept.at[unit, t, pl.ds((at + i) * BLK, BLK)]
            target = pairs.at[its_unit, t, pl.ds(pl.multiple_of(start + i * BLK, BLK), BLK)]
        return pltpu.make_async_remote_copy(
            source, target,
            kept_send.at[unit, segment], kept_recv.at[its_unit, segment],
            device_id=device, device_id_type=MESH,
        )

    def send_kept(unit):
        f = frame_of(unit)
        for t in range(2):
            stage[t] = pairs[unit, t, :S, :].reshape(NB, BLK, HD)
        for segment in ORDER:
            distance, direction, count, at = SEGMENTS[segment]
            there, here = inside(f, segment, unit)
            to = clipped(target_frame(f, segment))

            def chosen(i):
                keep = keeps[distance]
                return keep[i, direction, to] if count > 1 else keep[direction, i, to]

            @pl.when(there > 0)
            def _():
                for i in range(count):
                    block = chosen(i)
                    for t in range(2):
                        kept[unit, t, (at + i) * BLK : (at + i + 1) * BLK, :] = stage[t, block]
                for i in range(count):
                    for t in range(2):
                        kept_copy(segment, unit, (i, t)).start()

            if here is not None:
                start = first_block(to, segment)

                @pl.when(here > 0)
                def _():
                    for i in range(count):
                        block = chosen(i)
                        rows = pl.ds(pl.multiple_of((start + i) * BLK, BLK), BLK)
                        for t in range(2):
                            pairs[unit ^ 1, t, rows, :] = stage[t, block]

    def wait_kept(unit):
        f = frame_of(unit)
        for segment, (distance, direction, count, _) in enumerate(SEGMENTS):
            there = reaches(f, distance, direction)
            if distance == 2 and unit != 4:
                there = there * (1 - role_of(f) if direction == 0 else role_of(f))

            @pl.when(there > 0)
            def _():
                start = pl.multiple_of(first_block(f, segment) * BLK, BLK)
                target = pairs.at[unit, :, pl.ds(start, count * BLK)]
                pltpu.make_async_copy(target, target, kept_recv.at[unit, segment]).wait()

    def weigh(q, u, first, last, usable):
        scores = nt_dot(q, pairs[u, 0, first * BLK : last * BLK, :])
        parts = []
        for b in range(first, last):
            part = scores[:, (b - first) * BLK : (b - first + 1) * BLK]
            if b >= NB + 11:
                part = part + jnp.where(b < usable, 0.0, NEGATIVE)
            parts.append(part)
        peak = functools.reduce(jnp.maximum, parts)
        return parts, jnp.max(peak, axis=1, keepdims=True) * SCALE

    def gather(parts, above, u, first, last):
        weights = jnp.concatenate(
            [jnp.exp2(part * SCALE - above).astype(jnp.bfloat16) for part in parts], axis=1
        )
        wide = jnp.concatenate(
            [pairs[u, 1, first * BLK : last * BLK, :], jnp.ones(((last - first) * BLK, HD), jnp.bfloat16)], axis=1
        )
        product = jnp.dot(weights, wide, preferred_element_type=jnp.float32)
        return product[:, :HD], product[:, HD:]

    def tile_rows(i):
        return pl.ds(pl.multiple_of(i * TQ, TQ), TQ)

    def attend_own(u, n, i):
        rows = tile_rows(i)
        parts, peak = weigh(queries[u, rows, :], u, 0, NB, NB)
        above = jnp.broadcast_to(peak, (TQ, HD))
        running[n, 0, rows, :] = above
        running[n, 1, rows, :], running[n, 2, rows, :] = gather(parts, above, u, 0, NB)

    def attend_kept(u, n, i):
        rows = tile_rows(i)
        usable = first_block(frame_of(u), len(SEGMENTS)) + 1
        q = queries[u, rows, :]
        top, summed, total = running[n, 0, rows, :], running[n, 1, rows, :], running[n, 2, rows, :]
        for first, last in CHUNKS:
            parts, peak = weigh(q, u, first, last, usable)
            above = jnp.maximum(top, peak)
            fade = jnp.exp2(top - above)
            product, sums = gather(parts, above, u, first, last)
            summed = summed * fade + product
            total = total * fade + sums
            top = above
        heads_out[u, rows, :] = (summed / total).astype(jnp.bfloat16)

    def give_back(s, i):
        unit, lanes = unit_of(s, i), lanes_of(head_at(s, 0))
        source, target = heads_out.at[unit, rows_of(members[i % MEMBERS])], out_hbm.at[0, :, lanes]
        if i == 0:
            return pltpu.make_async_copy(source, target, own_sem.at[3, s])
        return pltpu.make_async_remote_copy(
            source, target, out_send.at[s, i], out_recv.at[s, i], device_id=place(i), device_id_type=MESH
        )

    def give(unit):
        for i in partners_of(unit):
            give_back(unit // 2, i).start()

    def take(*tensors):
        for t, unit in tensors:
            wait_exchange(t, unit)

    loads[0].wait()
    start_exchange(0, 0)
    loads[1].wait()
    normalise(k_in, k_gain, k_norm)
    start_exchange(1, 0)
    loads[2].wait()
    normalise(q_in, q_gain, q_norm)
    start_exchange(2, 0)
    for unit in range(1, UNITS):
        for t in range(3):
            start_exchange(t, unit)

    own, others = 0, 1
    values_keys = lambda unit: take((0, unit), (1, unit))

    def before_own_1():
        values_keys(1)
        send_kept(1)
        take((2, 1))

    def before_others_1():
        give(0)
        wait_kept(1)
        values_keys(2)
        send_kept(2)

    def late_others_1():
        values_keys(3)
        send_kept(3)

    def before_own_2():
        give(1)
        take((2, 2))

    def late_others_2():
        values_keys(4)
        send_kept(4)

    def before_others_3():
        give(2)
        wait_kept(3)

    def before_own_4():
        give(3)
        take((2, 4))

    values_keys(0)
    send_kept(0)
    phases = [
        (own, 0, 0, TILES, lambda: take((2, 0))),
        (own, 1, 0, TILES, before_own_1),
        (others, 0, 0, TILES, lambda: wait_kept(0)),
        (others, 1, 0, TILES - 1, before_others_1),
        (others, 1, TILES - 1, TILES, late_others_1),
        (own, 2, 0, TILES, before_own_2),
        (own, 3, 0, TILES, lambda: take((2, 3))),
        (others, 2, 0, 1, lambda: wait_kept(2)),
        (others, 2, 1, TILES, late_others_2),
        (others, 3, 0, TILES, before_others_3),
        (own, 4, 0, TILES, before_own_4),
        (others, 4, 0, TILES, lambda: wait_kept(4)),
    ]

    def pick(n, column):
        return functools.reduce(lambda v, k: jnp.where(n == k, phases[k][column], v), range(len(phases)), 0)

    def phase(n, carry):
        kind, unit, first, last = (pick(n, column) for column in range(4))
        for k, (_, _, _, _, todo) in enumerate(phases):
            if todo is not None:
                pl.when(n == k)(todo)

        def own_tile(i, c):
            attend_own(unit, unit, i)
            return c

        def kept_tile(i, c):
            attend_kept(unit, unit, i)
            return c

        lax.fori_loop(first, jnp.where(kind == own, last, first), own_tile, 0)
        lax.fori_loop(first, jnp.where(kind == own, first, last), kept_tile, 0)
        return carry

    lax.fori_loop(0, len(phases), phase, 0)
    give(4)

    for unit in range(UNITS):
        s = unit // 2
        for i in partners_of(unit):
            if i == 0:
                give_back(s, 0).wait()
                continue
            for t in range(3):
                exchange(t, s, i).wait_send()
            give_back(s, i).wait_send()
            target = out_hbm.at[0, :, lanes_of(head_at(s, i))]
            pltpu.make_async_copy(target, target, out_recv.at[s, i]).wait()
    for unit in range(UNITS):
        for segment in range(len(SEGMENTS)):
            @pl.when(inside(frame_of(unit), segment, unit)[0] > 0)
            def _():
                kept_copy(segment, unit).wait_send()


def on_device(q_in, k_in, v_in, q_gain, k_gain, keep_one, keep_two, keep_four, keep_eight):
    hbm = pl.BlockSpec(memory_space=pl.ANY)
    vmem = pl.BlockSpec(memory_space=pltpu.VMEM)
    smem = pl.BlockSpec(memory_space=pltpu.SMEM)
    bf16 = jnp.bfloat16
    dma = pltpu.SemaphoreType.DMA
    return pl.pallas_call(
        kernel,
        out_shape=jax.ShapeDtypeStruct((1, TOKENS, WIDTH), bf16),
        in_specs=[hbm, hbm, hbm, vmem, vmem, smem, smem, smem, smem],
        out_specs=hbm,
        scratch_shapes=[
            pltpu.VMEM((TOKENS, WIDTH), bf16),
            pltpu.VMEM((TOKENS, WIDTH), bf16),
            pltpu.VMEM((TOKENS, WIDTH), bf16),
            pltpu.VMEM((HEADS, TOKENS, HD), bf16),
            pltpu.VMEM((HEADS, TOKENS, HD), bf16),
            pltpu.VMEM((UNITS, S, HD), bf16),
            pltpu.VMEM((UNITS, 2, KEYS, HD), bf16),
            pltpu.VMEM((2, NB, BLK, HD), bf16),
            pltpu.VMEM((UNITS, 2, KEPT * BLK, HD), bf16),
            pltpu.VMEM((UNITS, S, HD), bf16),
            pltpu.VMEM((UNITS, 3, S, HD), jnp.float32),
            dma((3,)),
            dma((4, 3)),
            dma((3, 3, 2 * MEMBERS)),
            dma((3, 3, 2 * MEMBERS)),
            dma((UNITS, len(SEGMENTS))),
            dma((UNITS, len(SEGMENTS))),
            dma((3, 2 * MEMBERS)),
            dma((3, 2 * MEMBERS)),
        ],
        compiler_params=pltpu.CompilerParams(
            collective_id=0, has_side_effects=True, vmem_limit_bytes=60 * 2**20
        ),
        cost_estimate=pl.CostEstimate(
            flops=4 * S * KEYS * PER * HD, bytes_accessed=8 * TOKENS * WIDTH, transcendentals=S * KEYS * PER
        ),
        name="attend",
    )(
        q_in, k_in, v_in, q_gain.reshape(1, WIDTH), k_gain.reshape(1, WIDTH),
        keep_one.transpose(2, 1, 0), keep_two.transpose(2, 1, 0),
        keep_four.transpose(1, 2, 0), keep_eight.transpose(1, 2, 0),
    )


def solution(mesh):
    return jax.shard_map(
        on_device,
        mesh=mesh,
        in_specs=(P("tm", "head", None),) * 3 + (P(),) * 6,
        out_specs=P("tm", "head", None),
        check_vma=False,
    )
```

```python
import functools
import math

import jax
import jax.numpy as jnp
from jax import lax
from jax.experimental import pallas as pl
from jax.experimental.pallas import tpu as pltpu
from jax.sharding import PartitionSpec as P

MESH = pl.DeviceIdType.MESH
HEADS = 40
HD = 128
BLK = 128
EPSILON = 1e-06
NEGATIVE = -1e30
LOG2E = math.log2(math.e)

FRAMES = 16
MEMBERS = 8
PER = HEADS // MEMBERS
TOKENS = 192
S = TOKENS * MEMBERS
NB = S // BLK
WIDTH = HEADS * HD
SEGMENTS = ((1, 0, 6, 0), (1, 1, 6, 6), (2, 0, 3, 12), (2, 1, 3, 15), (4, 0, 1, 18), (4, 1, 1, 19), (8, 0, 1, 20), (8, 1, 1, 20))
KEPT = 21
UNITS = 5
ORDER = (0, 1, 2, 3, 4, 5, 6, 7)
KEYS = (NB + KEPT) * BLK
TQ = 512
TILES = S // TQ
CHUNKS = ((NB, NB + 11), (NB + 11, NB + KEPT))
SCALE = LOG2E / math.sqrt(HD)
NORM_ROWS = 32


def nt_dot(a, b):
    return lax.dot_general(a, b, (((1,), (1,)), ((), ())), preferred_element_type=jnp.float32)


def reaches(frame, distance, direction):
    room = frame if direction == 0 else FRAMES - 1 - frame
    return jnp.minimum(lax.div(room, distance), 1)


def first_block(frame, segment):
    at = NB
    for distance, direction, count, _ in SEGMENTS[:segment]:
        if distance < 8:
            at = at + count * reaches(frame, distance, direction)
    return at


def kernel(
    q_hbm, k_hbm, v_hbm, q_gain, k_gain, keep_one, keep_two, keep_four, keep_eight,
    out_hbm,
    q_in, k_in, v_in, q_norm, k_norm, queries, pairs, stage, kept, heads_out, running,
    load_sem, own_sem, a2a_send, a2a_recv, kept_send, kept_recv, out_send, out_recv,
):
    frame = lax.axis_index("tm")
    member = lax.axis_index("head")
    plane, role, core = lax.div(frame, 4), lax.rem(lax.div(frame, 2), 2), lax.rem(frame, 2)
    keeps = {1: keep_one, 2: keep_two, 4: keep_four, 8: keep_eight}

    def bit(m, b):
        return (m // b) % 2 if isinstance(m, int) else lax.rem(lax.div(m, b), 2)

    def flip(m, bits):
        total = 0
        for b in (1, 2, 4):
            x = bit(m, b) + bit(bits, b)
            total = total + b * lax.rem(x, 2)
        return total

    roles = [lax.rem(role + other, 2) for other in range(2)]
    members = [flip(member, j) for j in range(MEMBERS)]

    def place(i):
        return 4 * plane + 2 * roles[i // MEMBERS] + core, members[i % MEMBERS]

    def head_at(s, i):
        its_role = roles[i // MEMBERS]
        group = flip(members[i % MEMBERS], 4 * its_role)
        return group * PER + (2 * its_role + s if s < 2 else 4)

    def unit_of(s, i):
        return 2 * s + i // MEMBERS if s < 2 else 4

    def partners_of(unit):
        first = MEMBERS * (unit % 2)
        return range(first, first + MEMBERS)

    def frame_of(unit):
        return 4 * plane + 2 * ((role + unit % 2) % 2) + core

    def rows_of(m):
        return pl.ds(pl.multiple_of(m * TOKENS, 64), TOKENS)

    def lanes_of(head):
        return pl.ds(pl.multiple_of(head * HD, HD), HD)

    loads = [
        pltpu.make_async_copy(v_hbm.at[0], v_in, load_sem.at[0]),
        pltpu.make_async_copy(k_hbm.at[0], k_in, load_sem.at[1]),
        pltpu.make_async_copy(q_hbm.at[0], q_in, load_sem.at[2]),
    ]
    for load in loads:
        load.start()

    barrier = pltpu.get_barrier_semaphore()

    def greet(device):
        pl.semaphore_signal(barrier, inc=1, device_id=device, device_id_type=MESH)

    first_idle = (NB + 11) * BLK
    for u in range(UNITS):
        for t in range(2):
            pairs[u, t, first_idle:, :] = jnp.zeros((KEYS - first_idle, HD), jnp.bfloat16)

    for i in range(1, 2 * MEMBERS):
        greet(place(i))
    greet((frame + 1 - 2 * core, member))
    expected = 2 * MEMBERS
    near = jnp.minimum(3 - plane, 1), jnp.minimum(plane, 1)
    far = (3 - plane) // 2, plane // 2
    far = jnp.minimum(far[0], 1), jnp.minimum(far[1], 1)
    across = core * near[0] + (1 - core) * near[1]
    side = 2 * core - 1
    meets = [
        (near[0], frame + 4), (near[1], frame - 4), (far[0], frame + 8), (far[1], frame - 8),
        (across, frame + 4 * side - side),
    ]
    for there, to in meets:
        expected = expected + there

        @pl.when(there > 0)
        def _():
            greet((to, member))

    def target_frame(f, segment):
        distance, direction, _, _ = SEGMENTS[segment]
        return f + distance if direction == 0 else f - distance

    def clipped(f):
        return jnp.clip(f, 0, FRAMES - 1)

    def role_of(f):
        return lax.rem(lax.div(f, 2), 2)

    def single_place(to):
        return to, flip(member, 4 * ((role_of(to) + role) % 2))

    for segment, (distance, direction, _, _) in enumerate(SEGMENTS):
        to = target_frame(frame, segment)
        there = reaches(frame, distance, 1 - direction)
        expected = expected + there

        @pl.when(there > 0)
        def _():
            greet(single_place(clipped(to)))

    pl.semaphore_wait(barrier, expected)

    def exchange(t, s, i):
        head, unit = head_at(s, i), unit_of(s, i)
        if t == 0:
            source, target = v_in.at[:, lanes_of(head)], pairs.at[unit, 1, rows_of(member)]
        elif t == 1:
            source, target = k_norm.at[head], pairs.at[unit, 0, rows_of(member)]
        else:
            source, target = q_norm.at[head], queries.at[unit, rows_of(member)]
        if i == 0:
            return pltpu.make_async_copy(source, target, own_sem.at[t, s])
        return pltpu.make_async_remote_copy(
            source, target, a2a_send.at[t], a2a_recv.at[t, unit],
            device_id=place(i), device_id_type=MESH,
        )

    def start_exchange(t, unit):
        for i in partners_of(unit):
            exchange(t, unit // 2, i).start()

    def wait_exchange(t, unit):
        rows = S
        if unit % 2 == 0:
            exchange(t, unit // 2, 0).wait()
            rows = S - TOKENS
        some = heads_out.at[0, pl.ds(0, rows)]
        pltpu.make_async_copy(some, some, a2a_recv.at[t, unit]).wait()

    def normalise(source, gain, target):
        scale = gain[...]

        def some_rows(i, carry):
            rows = pl.ds(pl.multiple_of(i * NORM_ROWS, NORM_ROWS), NORM_ROWS)
            wide = source[rows, :].astype(jnp.float32)
            meansq = jnp.mean(wide * wide, axis=-1, keepdims=True)
            normed = (wide * lax.rsqrt(meansq + EPSILON) * scale).astype(jnp.bfloat16)
            for head in range(HEADS):
                target[head, rows, :] = normed[:, head * HD : (head + 1) * HD]
            return carry

        lax.fori_loop(0, TOKENS // NORM_ROWS, some_rows, 0)

    def inside(f, segment, unit):
        distance, direction, _, _ = SEGMENTS[segment]
        there = reaches(f, distance, 1 - direction)
        if distance != 2 or unit == 4:
            return there, None
        here = 1 - role_of(f) if direction == 0 else role_of(f)
        return there * (1 - here), here

    def kept_copy(segment, unit):
        _, _, count, at = SEGMENTS[segment]
        to = clipped(target_frame(frame_of(unit), segment))
        start = pl.multiple_of(first_block(to, segment) * BLK, BLK)
        if unit == 4:
            device, its_unit = single_place(to), 4
        else:
            device = (4 * (to // 4) + 2 * role + to % 2, member)
            its_unit = 2 * (unit // 2) + (role_of(to) + role) % 2
        source, target = kept.at[unit, :, pl.ds(at * BLK, count * BLK)], pairs.at[its_unit, :, pl.ds(start, count * BLK)]
        return pltpu.make_async_remote_copy(
            source, target,
            kept_send.at[unit, segment], kept_recv.at[its_unit, segment],
            device_id=device, device_id_type=MESH,
        )

    def send_kept(unit):
        f = frame_of(unit)
        for t in range(2):
            stage[t] = pairs[unit, t, :S, :].reshape(NB, BLK, HD)
        for segment in ORDER:
            distance, direction, count, at = SEGMENTS[segment]
            there, here = inside(f, segment, unit)
            to = clipped(target_frame(f, segment))

            def chosen(i):
                keep = keeps[distance]
                return keep[i, direction, to] if count > 1 else keep[direction, i, to]

            @pl.when(there > 0)
            def _():
                for i in range(count):
                    block = chosen(i)
                    for t in range(2):
                        kept[unit, t, (at + i) * BLK : (at + i + 1) * BLK, :] = stage[t, block]
                kept_copy(segment, unit).start()

            if here is not None:
                start = first_block(to, segment)

                @pl.when(here > 0)
                def _():
                    for i in range(count):
                        block = chosen(i)
                        rows = pl.ds(pl.multiple_of((start + i) * BLK, BLK), BLK)
                        for t in range(2):
                            pairs[unit ^ 1, t, rows, :] = stage[t, block]

    def wait_kept(unit):
        f = frame_of(unit)
        for segment, (distance, direction, count, _) in enumerate(SEGMENTS):
            there = reaches(f, distance, direction)
            if distance == 2 and unit != 4:
                there = there * (1 - role_of(f) if direction == 0 else role_of(f))

            @pl.when(there > 0)
            def _():
                start = pl.multiple_of(first_block(f, segment) * BLK, BLK)
                target = pairs.at[unit, :, pl.ds(start, count * BLK)]
                pltpu.make_async_copy(target, target, kept_recv.at[unit, segment]).wait()

    def weigh(q, u, first, last, usable):
        scores = nt_dot(q, pairs[u, 0, first * BLK : last * BLK, :])
        parts = []
        for b in range(first, last):
            part = scores[:, (b - first) * BLK : (b - first + 1) * BLK]
            if b >= NB + 11:
                part = part + jnp.where(b < usable, 0.0, NEGATIVE)
            parts.append(part)
        peak = functools.reduce(jnp.maximum, parts)
        return parts, jnp.max(peak, axis=1, keepdims=True) * SCALE

    def gather(parts, above, u, first, last):
        weights = jnp.concatenate(
            [jnp.exp2(part * SCALE - above).astype(jnp.bfloat16) for part in parts], axis=1
        )
        wide = jnp.concatenate(
            [pairs[u, 1, first * BLK : last * BLK, :], jnp.ones(((last - first) * BLK, HD), jnp.bfloat16)], axis=1
        )
        product = jnp.dot(weights, wide, preferred_element_type=jnp.float32)
        return product[:, :HD], product[:, HD:]

    def tile_rows(i):
        return pl.ds(pl.multiple_of(i * TQ, TQ), TQ)

    def attend_own(u, n, i):
        rows = tile_rows(i)
        parts, peak = weigh(queries[u, rows, :], u, 0, NB, NB)
        above = jnp.broadcast_to(peak, (TQ, HD))
        running[n, 0, rows, :] = above
        running[n, 1, rows, :], running[n, 2, rows, :] = gather(parts, above, u, 0, NB)

    def attend_kept(u, n, i):
        rows = tile_rows(i)
        usable = first_block(frame_of(u), len(SEGMENTS)) + 1
        q = queries[u, rows, :]
        top, summed, total = running[n, 0, rows, :], running[n, 1, rows, :], running[n, 2, rows, :]
        for first, last in CHUNKS:
            parts, peak = weigh(q, u, first, last, usable)
            above = jnp.maximum(top, peak)
            fade = jnp.exp2(top - above)
            product, sums = gather(parts, above, u, first, last)
            summed = summed * fade + product
            total = total * fade + sums
            top = above
        heads_out[u, rows, :] = (summed / total).astype(jnp.bfloat16)

    def give_back(s, i):
        unit, lanes = unit_of(s, i), lanes_of(head_at(s, 0))
        source, target = heads_out.at[unit, rows_of(members[i % MEMBERS])], out_hbm.at[0, :, lanes]
        if i == 0:
            return pltpu.make_async_copy(source, target, own_sem.at[3, s])
        return pltpu.make_async_remote_copy(
            source, target, out_send.at[0], out_recv.at[0], device_id=place(i), device_id_type=MESH
        )

    def give(unit):
        for i in partners_of(unit):
            give_back(unit // 2, i).start()

    def take(*tensors):
        for t, unit in tensors:
            wait_exchange(t, unit)

    def give_rows(unit, first, last):
        s, other = unit // 2, unit % 2
        for m in range(first, last):
            j = flip(member, m)
            source = heads_out.at[unit, m * TOKENS : (m + 1) * TOKENS]
            target = out_hbm.at[0, :, lanes_of(head_at(s, 0))]

            def send():
                pltpu.make_async_remote_copy(
                    source, target, out_send.at[0], out_recv.at[0],
                    device_id=(4 * plane + 2 * roles[other] + core, m), device_id_type=MESH,
                ).start()

            if other:
                send()
                continue
            pl.when(j > 0)(send)

            @pl.when(j == 0)
            def _():
                pltpu.make_async_copy(source, target, own_sem.at[3, s]).start()

    loads[0].wait()
    start_exchange(0, 4)
    start_exchange(0, 1)
    loads[1].wait()
    normalise(k_in, k_gain, k_norm)
    start_exchange(1, 4)
    start_exchange(1, 1)
    loads[2].wait()
    normalise(q_in, q_gain, q_norm)
    start_exchange(2, 4)
    start_exchange(2, 1)
    for t in range(3):
        start_exchange(t, 0)
    take((0, 4), (1, 4))
    send_kept(4)
    for unit in (3, 2):
        for t in range(3):
            start_exchange(t, unit)

    own, others = 0, 1
    values_keys = lambda unit: take((0, unit), (1, unit))

    def before_own(unit):
        values_keys(unit)
        send_kept(unit)
        take((2, unit))

    def before_others(unit, done):
        give(done)
        wait_kept(unit)

    def meanwhile(unit):
        values_keys(unit)
        send_kept(unit)

    def before_own_3():
        give(0)
        take((2, 3))

    phases = [
        (own, 4, 0, TILES, lambda: take((2, 4))),
        (own, 1, 0, TILES, lambda: before_own(1)),
        (own, 0, 0, TILES, lambda: before_own(0)),
        (others, 4, 0, TILES, lambda: wait_kept(4)),
        (others, 1, 0, 1, lambda: before_others(1, 4)),
        (others, 1, 1, TILES, lambda: meanwhile(3)),
        (others, 0, 0, 1, lambda: before_others(0, 1)),
        (others, 0, 1, TILES, lambda: meanwhile(2)),
        (own, 3, 0, TILES, before_own_3),
        (own, 2, 0, TILES, lambda: take((2, 2))),
        (others, 3, 0, TILES, lambda: wait_kept(3)),
        (others, 2, 0, 1, lambda: before_others(2, 3)),
        (others, 2, 1, 2, lambda: give_rows(2, 0, 2)),
        (others, 2, 2, TILES, lambda: give_rows(2, 2, 5)),
    ]

    def pick(n, column):
        return functools.reduce(lambda v, k: jnp.where(n == k, phases[k][column], v), range(len(phases)), 0)

    def phase(n, carry):
        kind, unit, first, last = (pick(n, column) for column in range(4))
        for k, (_, _, _, _, todo) in enumerate(phases):
            if todo is not None:
                pl.when(n == k)(todo)

        def own_tile(i, c):
            attend_own(unit, unit, i)
            return c

        def kept_tile(i, c):
            attend_kept(unit, unit, i)
            return c

        lax.fori_loop(first, jnp.where(kind == own, last, first), own_tile, 0)
        lax.fori_loop(first, jnp.where(kind == own, first, last), kept_tile, 0)
        return carry

    lax.fori_loop(0, len(phases), phase, 0)
    give_rows(2, 5, 8)

    for s in range(3):
        give_back(s, 0).wait()
    copies = k_norm.at[pl.ds(0, MEMBERS * UNITS - 3)]
    for semaphore in (a2a_send.at[0], a2a_send.at[1], a2a_send.at[2], out_send.at[0], out_recv.at[0]):
        pltpu.make_async_copy(copies, copies, semaphore).wait()
    for unit in range(UNITS):
        for segment in range(len(SEGMENTS)):
            @pl.when(inside(frame_of(unit), segment, unit)[0] > 0)
            def _():
                kept_copy(segment, unit).wait_send()


def on_device(q_in, k_in, v_in, q_gain, k_gain, keep_one, keep_two, keep_four, keep_eight):
    hbm = pl.BlockSpec(memory_space=pl.ANY)
    vmem = pl.BlockSpec(memory_space=pltpu.VMEM)
    smem = pl.BlockSpec(memory_space=pltpu.SMEM)
    bf16 = jnp.bfloat16
    dma = pltpu.SemaphoreType.DMA
    return pl.pallas_call(
        kernel,
        out_shape=jax.ShapeDtypeStruct((1, TOKENS, WIDTH), bf16),
        in_specs=[hbm, hbm, hbm, vmem, vmem, smem, smem, smem, smem],
        out_specs=hbm,
        scratch_shapes=[
            pltpu.VMEM((TOKENS, WIDTH), bf16),
            pltpu.VMEM((TOKENS, WIDTH), bf16),
            pltpu.VMEM((TOKENS, WIDTH), bf16),
            pltpu.VMEM((HEADS, TOKENS, HD), bf16),
            pltpu.VMEM((HEADS, TOKENS, HD), bf16),
            pltpu.VMEM((UNITS, S, HD), bf16),
            pltpu.VMEM((UNITS, 2, KEYS, HD), bf16),
            pltpu.VMEM((2, NB, BLK, HD), bf16),
            pltpu.VMEM((UNITS, 2, KEPT * BLK, HD), bf16),
            pltpu.VMEM((UNITS, S, HD), bf16),
            pltpu.VMEM((UNITS, 3, S, HD), jnp.float32),
            dma((3,)),
            dma((4, 3)),
            dma((3,)),
            dma((3, UNITS)),
            dma((UNITS, len(SEGMENTS))),
            dma((UNITS, len(SEGMENTS))),
            dma((1,)),
            dma((1,)),
        ],
        compiler_params=pltpu.CompilerParams(
            collective_id=0, has_side_effects=True, vmem_limit_bytes=60 * 2**20
        ),
        cost_estimate=pl.CostEstimate(
            flops=4 * S * KEYS * PER * HD, bytes_accessed=8 * TOKENS * WIDTH, transcendentals=S * KEYS * PER
        ),
        name="attend",
    )(
        q_in, k_in, v_in, q_gain.reshape(1, WIDTH), k_gain.reshape(1, WIDTH),
        keep_one.transpose(2, 1, 0), keep_two.transpose(2, 1, 0),
        keep_four.transpose(1, 2, 0), keep_eight.transpose(1, 2, 0),
    )


def solution(mesh):
    return jax.shard_map(
        on_device,
        mesh=mesh,
        in_specs=(P("tm", "head", None),) * 3 + (P(),) * 6,
        out_specs=P("tm", "head", None),
        check_vma=False,
    )
```

```python
import functools
import math

import jax
import jax.numpy as jnp
from jax import lax
from jax.experimental import pallas as pl
from jax.experimental.pallas import tpu as pltpu
from jax.sharding import PartitionSpec as P

MESH = pl.DeviceIdType.MESH
HEADS = 40
HD = 128
BLK = 128
EPSILON = 1e-06
NEGATIVE = -1e30
LOG2E = math.log2(math.e)

FRAMES = 16
MEMBERS = 8
PER = HEADS // MEMBERS
TOKENS = 192
S = TOKENS * MEMBERS
NB = S // BLK
WIDTH = HEADS * HD
SEGMENTS = ((1, 0, 6, 0), (1, 1, 6, 6), (2, 0, 3, 12), (2, 1, 3, 15), (4, 0, 1, 18), (4, 1, 1, 19), (8, 0, 1, 20), (8, 1, 1, 20))
KEPT = 21
UNITS = 5
ORDER = (0, 1, 2, 3, 4, 5, 6, 7)
KEYS = (NB + KEPT) * BLK
TQ = 768
TILES = S // TQ
CHUNKS = ((NB, NB + 11), (NB + 11, NB + KEPT))
SCALE = LOG2E / math.sqrt(HD)
NORM_ROWS = 32


def nt_dot(a, b):
    return lax.dot_general(a, b, (((1,), (1,)), ((), ())), preferred_element_type=jnp.float32)


def reaches(frame, distance, direction):
    room = frame if direction == 0 else FRAMES - 1 - frame
    return jnp.minimum(lax.div(room, distance), 1)


def first_block(frame, segment):
    at = NB
    for distance, direction, count, _ in SEGMENTS[:segment]:
        if distance < 8:
            at = at + count * reaches(frame, distance, direction)
    return at


def kernel(
    q_hbm, k_hbm, v_hbm, q_gain, k_gain, keep_one, keep_two, keep_four, keep_eight,
    out_hbm,
    q_in, k_in, q_norm, k_norm, queries, pairs, stage, kept, heads_out, running,
    load_sem, own_sem, a2a_send, a2a_recv, kept_send, kept_recv, out_send, out_recv,
):
    frame = lax.axis_index("tm")
    member = lax.axis_index("head")
    plane, role, core = lax.div(frame, 4), lax.rem(lax.div(frame, 2), 2), lax.rem(frame, 2)
    keeps = {1: keep_one, 2: keep_two, 4: keep_four, 8: keep_eight}

    def bit(m, b):
        return (m // b) % 2 if isinstance(m, int) else lax.rem(lax.div(m, b), 2)

    def flip(m, bits):
        total = 0
        for b in (1, 2, 4):
            x = bit(m, b) + bit(bits, b)
            total = total + b * lax.rem(x, 2)
        return total

    roles = [lax.rem(role + other, 2) for other in range(2)]
    members = [flip(member, j) for j in range(MEMBERS)]

    def place(i):
        return 4 * plane + 2 * roles[i // MEMBERS] + core, members[i % MEMBERS]

    def head_at(s, i):
        its_role = roles[i // MEMBERS]
        group = flip(members[i % MEMBERS], 4 * its_role)
        return group * PER + (2 * its_role + s if s < 2 else 4)

    def unit_of(s, i):
        return 2 * s + i // MEMBERS if s < 2 else 4

    def partners_of(unit):
        first = MEMBERS * (unit % 2)
        return range(first, first + MEMBERS)

    def frame_of(unit):
        return 4 * plane + 2 * ((role + unit % 2) % 2) + core

    def rows_of(m):
        return pl.ds(pl.multiple_of(m * TOKENS, 64), TOKENS)

    def lanes_of(head):
        return pl.ds(pl.multiple_of(head * HD, HD), HD)

    loads = [
        pltpu.make_async_copy(k_hbm.at[0], k_in, load_sem.at[0]),
        pltpu.make_async_copy(q_hbm.at[0], q_in, load_sem.at[1]),
    ]
    for load in loads:
        load.start()

    barrier = pltpu.get_barrier_semaphore()

    def greet(device):
        pl.semaphore_signal(barrier, inc=1, device_id=device, device_id_type=MESH)

    first_idle = (NB + 11) * BLK
    for u in range(UNITS):
        for t in range(2):
            pairs[u, t, first_idle:, :] = jnp.zeros((KEYS - first_idle, HD), jnp.bfloat16)

    for i in range(1, 2 * MEMBERS):
        greet(place(i))
    greet((frame + 1 - 2 * core, member))
    expected = 2 * MEMBERS
    near = jnp.minimum(3 - plane, 1), jnp.minimum(plane, 1)
    far = (3 - plane) // 2, plane // 2
    far = jnp.minimum(far[0], 1), jnp.minimum(far[1], 1)
    across = core * near[0] + (1 - core) * near[1]
    side = 2 * core - 1
    meets = [
        (near[0], frame + 4), (near[1], frame - 4), (far[0], frame + 8), (far[1], frame - 8),
        (across, frame + 4 * side - side),
    ]
    for there, to in meets:
        expected = expected + there

        @pl.when(there > 0)
        def _():
            greet((to, member))

    def target_frame(f, segment):
        distance, direction, _, _ = SEGMENTS[segment]
        return f + distance if direction == 0 else f - distance

    def clipped(f):
        return jnp.clip(f, 0, FRAMES - 1)

    def role_of(f):
        return lax.rem(lax.div(f, 2), 2)

    def single_place(to):
        return to, flip(member, 4 * ((role_of(to) + role) % 2))

    for segment, (distance, direction, _, _) in enumerate(SEGMENTS):
        to = target_frame(frame, segment)
        there = reaches(frame, distance, 1 - direction)
        expected = expected + there

        @pl.when(there > 0)
        def _():
            greet(single_place(clipped(to)))

    pl.semaphore_wait(barrier, expected)

    def exchange(t, s, i):
        head, unit = head_at(s, i), unit_of(s, i)
        if t == 0:
            source, target = v_hbm.at[0, :, lanes_of(head)], pairs.at[unit, 1, rows_of(member)]
        elif t == 1:
            source, target = k_norm.at[head], pairs.at[unit, 0, rows_of(member)]
        else:
            source, target = q_norm.at[head], queries.at[unit, rows_of(member)]
        if i == 0:
            return pltpu.make_async_copy(source, target, own_sem.at[t, s])
        return pltpu.make_async_remote_copy(
            source, target, a2a_send.at[t], a2a_recv.at[t, unit],
            device_id=place(i), device_id_type=MESH,
        )

    def start_exchange(t, unit):
        for i in partners_of(unit):
            exchange(t, unit // 2, i).start()

    def wait_exchange(t, unit):
        rows = S
        if unit % 2 == 0:
            exchange(t, unit // 2, 0).wait()
            rows = S - TOKENS
        some = heads_out.at[0, pl.ds(0, rows)]
        pltpu.make_async_copy(some, some, a2a_recv.at[t, unit]).wait()

    def normalise(source, gain, target):
        scale = gain[...]

        def some_rows(i, carry):
            rows = pl.ds(pl.multiple_of(i * NORM_ROWS, NORM_ROWS), NORM_ROWS)
            wide = source[rows, :].astype(jnp.float32)
            meansq = jnp.mean(wide * wide, axis=-1, keepdims=True)
            normed = (wide * lax.rsqrt(meansq + EPSILON) * scale).astype(jnp.bfloat16)
            for head in range(HEADS):
                target[head, rows, :] = normed[:, head * HD : (head + 1) * HD]
            return carry

        lax.fori_loop(0, TOKENS // NORM_ROWS, some_rows, 0)

    def inside(f, segment, unit):
        distance, direction, _, _ = SEGMENTS[segment]
        there = reaches(f, distance, 1 - direction)
        if distance != 2 or unit == 4:
            return there, None
        here = 1 - role_of(f) if direction == 0 else role_of(f)
        return there * (1 - here), here

    def kept_copy(segment, unit):
        _, _, count, at = SEGMENTS[segment]
        to = clipped(target_frame(frame_of(unit), segment))
        start = pl.multiple_of(first_block(to, segment) * BLK, BLK)
        if unit == 4:
            device, its_unit = single_place(to), 4
        else:
            device = (4 * (to // 4) + 2 * role + to % 2, member)
            its_unit = 2 * (unit // 2) + (role_of(to) + role) % 2
        source, target = kept.at[unit, :, pl.ds(at * BLK, count * BLK)], pairs.at[its_unit, :, pl.ds(start, count * BLK)]
        return pltpu.make_async_remote_copy(
            source, target,
            kept_send.at[unit, segment], kept_recv.at[its_unit, segment],
            device_id=device, device_id_type=MESH,
        )

    def send_kept(unit):
        f = frame_of(unit)
        for t in range(2):
            stage[t] = pairs[unit, t, :S, :].reshape(NB, BLK, HD)
        for segment in ORDER:
            distance, direction, count, at = SEGMENTS[segment]
            there, here = inside(f, segment, unit)
            to = clipped(target_frame(f, segment))

            def chosen(i):
                keep = keeps[distance]
                return keep[i, direction, to] if count > 1 else keep[direction, i, to]

            @pl.when(there > 0)
            def _():
                for i in range(count):
                    block = chosen(i)
                    for t in range(2):
                        kept[unit, t, (at + i) * BLK : (at + i + 1) * BLK, :] = stage[t, block]
                kept_copy(segment, unit).start()

            if here is not None:
                start = first_block(to, segment)

                @pl.when(here > 0)
                def _():
                    for i in range(count):
                        block = chosen(i)
                        rows = pl.ds(pl.multiple_of((start + i) * BLK, BLK), BLK)
                        for t in range(2):
                            pairs[unit ^ 1, t, rows, :] = stage[t, block]

    def wait_kept(unit):
        f = frame_of(unit)
        for segment, (distance, direction, count, _) in enumerate(SEGMENTS):
            there = reaches(f, distance, direction)
            if distance == 2 and unit != 4:
                there = there * (1 - role_of(f) if direction == 0 else role_of(f))

            @pl.when(there > 0)
            def _():
                start = pl.multiple_of(first_block(f, segment) * BLK, BLK)
                target = pairs.at[unit, :, pl.ds(start, count * BLK)]
                pltpu.make_async_copy(target, target, kept_recv.at[unit, segment]).wait()

    def weigh(q, u, first, last, usable):
        scores = nt_dot(q, pairs[u, 0, first * BLK : last * BLK, :])
        parts = []
        for b in range(first, last):
            part = scores[:, (b - first) * BLK : (b - first + 1) * BLK]
            if b >= NB + 11:
                part = part + jnp.where(b < usable, 0.0, NEGATIVE)
            parts.append(part)
        peak = functools.reduce(jnp.maximum, parts)
        return parts, jnp.max(peak, axis=1, keepdims=True) * SCALE

    def gather(parts, above, u, first, last):
        weights = jnp.concatenate(
            [jnp.exp2(part * SCALE - above).astype(jnp.bfloat16) for part in parts], axis=1
        )
        wide = jnp.concatenate(
            [pairs[u, 1, first * BLK : last * BLK, :], jnp.ones(((last - first) * BLK, HD), jnp.bfloat16)], axis=1
        )
        product = jnp.dot(weights, wide, preferred_element_type=jnp.float32)
        return product[:, :HD], product[:, HD:]

    def tile_rows(i):
        return pl.ds(pl.multiple_of(i * TQ, TQ), TQ)

    def attend_own(u, n, i):
        rows = tile_rows(i)
        parts, peak = weigh(queries[u, rows, :], u, 0, NB, NB)
        above = jnp.broadcast_to(peak, (TQ, HD))
        running[n, 0, rows, :] = above
        running[n, 1, rows, :], running[n, 2, rows, :] = gather(parts, above, u, 0, NB)

    def attend_kept(u, n, i):
        rows = tile_rows(i)
        usable = first_block(frame_of(u), len(SEGMENTS)) + 1
        q = queries[u, rows, :]
        top, summed, total = running[n, 0, rows, :], running[n, 1, rows, :], running[n, 2, rows, :]
        for first, last in CHUNKS:
            parts, peak = weigh(q, u, first, last, usable)
            above = jnp.maximum(top, peak)
            fade = jnp.exp2(top - above)
            product, sums = gather(parts, above, u, first, last)
            summed = summed * fade + product
            total = total * fade + sums
            top = above
        heads_out[u, rows, :] = (summed / total).astype(jnp.bfloat16)

    def give_back(s, i):
        unit, lanes = unit_of(s, i), lanes_of(head_at(s, 0))
        source, target = heads_out.at[unit, rows_of(members[i % MEMBERS])], out_hbm.at[0, :, lanes]
        if i == 0:
            return pltpu.make_async_copy(source, target, own_sem.at[3, s])
        return pltpu.make_async_remote_copy(
            source, target, out_send.at[0], out_recv.at[0], device_id=place(i), device_id_type=MESH
        )

    def give(unit):
        for i in partners_of(unit):
            give_back(unit // 2, i).start()

    def take(*tensors):
        for t, unit in tensors:
            wait_exchange(t, unit)

    def give_rows(unit, first, last):
        s, other = unit // 2, unit % 2
        for m in range(first, last):
            j = flip(member, m)
            source = heads_out.at[unit, m * TOKENS : (m + 1) * TOKENS]
            target = out_hbm.at[0, :, lanes_of(head_at(s, 0))]

            def send():
                pltpu.make_async_remote_copy(
                    source, target, out_send.at[0], out_recv.at[0],
                    device_id=(4 * plane + 2 * roles[other] + core, m), device_id_type=MESH,
                ).start()

            if other:
                send()
                continue
            pl.when(j > 0)(send)

            @pl.when(j == 0)
            def _():
                pltpu.make_async_copy(source, target, own_sem.at[3, s]).start()

    start_exchange(0, 4)
    start_exchange(0, 1)
    loads[0].wait()
    normalise(k_in, k_gain, k_norm)
    start_exchange(1, 4)
    start_exchange(1, 1)
    loads[1].wait()
    normalise(q_in, q_gain, q_norm)
    start_exchange(2, 4)
    start_exchange(2, 1)
    for t in range(3):
        start_exchange(t, 0)
    take((0, 4), (1, 4))
    send_kept(4)
    for unit in (3, 2):
        for t in range(3):
            start_exchange(t, unit)

    own, others = 0, 1
    values_keys = lambda unit: take((0, unit), (1, unit))

    def before_own(unit):
        values_keys(unit)
        send_kept(unit)
        take((2, unit))

    def before_others(unit, done):
        give(done)
        wait_kept(unit)

    def meanwhile(unit):
        values_keys(unit)
        send_kept(unit)

    def before_own_3():
        give(0)
        take((2, 3))

    phases = [
        (own, 4, 0, TILES, lambda: take((2, 4))),
        (own, 1, 0, TILES, lambda: before_own(1)),
        (own, 0, 0, TILES, lambda: before_own(0)),
        (others, 4, 0, TILES, lambda: wait_kept(4)),
        (others, 1, 0, 1, lambda: before_others(1, 4)),
        (others, 1, 1, TILES, lambda: meanwhile(3)),
        (others, 0, 0, 1, lambda: before_others(0, 1)),
        (others, 0, 1, TILES, lambda: meanwhile(2)),
        (own, 3, 0, TILES, before_own_3),
        (own, 2, 0, TILES, lambda: take((2, 2))),
        (others, 3, 0, TILES, lambda: wait_kept(3)),
        (others, 2, 0, 1, lambda: before_others(2, 3)),
        (others, 2, 1, TILES, lambda: give_rows(2, 0, 4)),
    ]

    def pick(n, column):
        return functools.reduce(lambda v, k: jnp.where(n == k, phases[k][column], v), range(len(phases)), 0)

    def phase(n, carry):
        kind, unit, first, last = (pick(n, column) for column in range(4))
        for k, (_, _, _, _, todo) in enumerate(phases):
            if todo is not None:
                pl.when(n == k)(todo)

        def own_tile(i, c):
            attend_own(unit, unit, i)
            return c

        def kept_tile(i, c):
            attend_kept(unit, unit, i)
            return c

        lax.fori_loop(first, jnp.where(kind == own, last, first), own_tile, 0)
        lax.fori_loop(first, jnp.where(kind == own, first, last), kept_tile, 0)
        return carry

    lax.fori_loop(0, len(phases), phase, 0)
    give_rows(2, 4, 8)

    for s in range(3):
        give_back(s, 0).wait()
    copies = k_norm.at[pl.ds(0, MEMBERS * UNITS - 3)]
    for semaphore in (a2a_send.at[0], a2a_send.at[1], a2a_send.at[2], out_send.at[0], out_recv.at[0]):
        pltpu.make_async_copy(copies, copies, semaphore).wait()
    for unit in range(UNITS):
        for segment in range(len(SEGMENTS)):
            @pl.when(inside(frame_of(unit), segment, unit)[0] > 0)
            def _():
                kept_copy(segment, unit).wait_send()


def on_device(q_in, k_in, v_in, q_gain, k_gain, keep_one, keep_two, keep_four, keep_eight):
    hbm = pl.BlockSpec(memory_space=pl.ANY)
    vmem = pl.BlockSpec(memory_space=pltpu.VMEM)
    smem = pl.BlockSpec(memory_space=pltpu.SMEM)
    bf16 = jnp.bfloat16
    dma = pltpu.SemaphoreType.DMA
    return pl.pallas_call(
        kernel,
        out_shape=pltpu.VMEM((1, TOKENS, WIDTH), bf16),
        in_specs=[hbm, hbm, hbm, vmem, vmem, smem, smem, smem, smem],
        out_specs=vmem,
        scratch_shapes=[
            pltpu.VMEM((TOKENS, WIDTH), bf16),
            pltpu.VMEM((TOKENS, WIDTH), bf16),
            pltpu.VMEM((HEADS, TOKENS, HD), bf16),
            pltpu.VMEM((HEADS, TOKENS, HD), bf16),
            pltpu.VMEM((UNITS, S, HD), bf16),
            pltpu.VMEM((UNITS, 2, KEYS, HD), bf16),
            pltpu.VMEM((2, NB, BLK, HD), bf16),
            pltpu.VMEM((UNITS, 2, KEPT * BLK, HD), bf16),
            pltpu.VMEM((UNITS, S, HD), bf16),
            pltpu.VMEM((UNITS, 3, S, HD), jnp.float32),
            dma((2,)),
            dma((4, 3)),
            dma((3,)),
            dma((3, UNITS)),
            dma((UNITS, len(SEGMENTS))),
            dma((UNITS, len(SEGMENTS))),
            dma((1,)),
            dma((1,)),
        ],
        compiler_params=pltpu.CompilerParams(
            collective_id=0, has_side_effects=True, vmem_limit_bytes=56 * 2**20
        ),
        cost_estimate=pl.CostEstimate(
            flops=4 * S * KEYS * PER * HD, bytes_accessed=8 * TOKENS * WIDTH, transcendentals=S * KEYS * PER
        ),
        name="attend",
    )(
        q_in, k_in, v_in, q_gain.reshape(1, WIDTH), k_gain.reshape(1, WIDTH),
        keep_one.transpose(2, 1, 0), keep_two.transpose(2, 1, 0),
        keep_four.transpose(1, 2, 0), keep_eight.transpose(1, 2, 0),
    )


def solution(mesh):
    return jax.shard_map(
        on_device,
        mesh=mesh,
        in_specs=(P("tm", "head", None),) * 3 + (P(),) * 6,
        out_specs=P("tm", "head", None),
        check_vma=False,
    )
```

```python
import functools
import math

import jax
import jax.numpy as jnp
from jax import lax
from jax.experimental import pallas as pl
from jax.experimental.pallas import tpu as pltpu
from jax.sharding import PartitionSpec as P

MESH = pl.DeviceIdType.MESH
HEADS = 40
HD = 128
BLK = 128
EPSILON = 1e-06
NEGATIVE = -1e30
LOG2E = math.log2(math.e)

FRAMES = 16
MEMBERS = 8
PER = HEADS // MEMBERS
TOKENS = 192
S = TOKENS * MEMBERS
NB = S // BLK
WIDTH = HEADS * HD
SEGMENTS = ((1, 0, 6, 0), (1, 1, 6, 6), (2, 0, 3, 12), (2, 1, 3, 15), (4, 0, 1, 18), (4, 1, 1, 19), (8, 0, 1, 20), (8, 1, 1, 20))
KEPT = 21
UNITS = 5
ORDER = (0, 1, 2, 3, 4, 5, 6, 7)
KEYS = (NB + KEPT) * BLK
TQ = 768
TILES = S // TQ
CHUNKS = ((NB, NB + 11), (NB + 11, NB + KEPT))
SCALE = LOG2E / math.sqrt(HD)
NORM_ROWS = 32


def nt_dot(a, b):
    return lax.dot_general(a, b, (((1,), (1,)), ((), ())), preferred_element_type=jnp.float32)


def reaches(frame, distance, direction):
    room = frame if direction == 0 else FRAMES - 1 - frame
    return jnp.minimum(lax.div(room, distance), 1)


def first_block(frame, segment):
    at = NB
    for distance, direction, count, _ in SEGMENTS[:segment]:
        if distance < 8:
            at = at + count * reaches(frame, distance, direction)
    return at


def kernel(
    q_hbm, k_hbm, v_hbm, q_gain, k_gain, keep_one, keep_two, keep_four, keep_eight,
    out_hbm,
    q_in, k_in, q_norm, k_norm, queries, pairs, stage, kept, heads_out, running,
    load_sem, own_sem, a2a_send, a2a_recv, kept_send, kept_recv, out_send, out_recv,
):
    frame = lax.axis_index("tm")
    member = lax.axis_index("head")
    plane, role, core = lax.div(frame, 4), lax.rem(lax.div(frame, 2), 2), lax.rem(frame, 2)
    keeps = {1: keep_one, 2: keep_two, 4: keep_four, 8: keep_eight}

    def bit(m, b):
        return (m // b) % 2 if isinstance(m, int) else lax.rem(lax.div(m, b), 2)

    def flip(m, bits):
        total = 0
        for b in (1, 2, 4):
            x = bit(m, b) + bit(bits, b)
            total = total + b * lax.rem(x, 2)
        return total

    roles = [lax.rem(role + other, 2) for other in range(2)]
    members = [flip(member, j) for j in range(MEMBERS)]

    def place(i):
        return 4 * plane + 2 * roles[i // MEMBERS] + core, members[i % MEMBERS]

    def head_at(s, i):
        its_role = roles[i // MEMBERS]
        group = flip(members[i % MEMBERS], 4 * its_role)
        return group * PER + (2 * its_role + s if s < 2 else 4)

    def unit_of(s, i):
        return 2 * s + i // MEMBERS if s < 2 else 4

    def partners_of(unit):
        first = MEMBERS * (unit % 2)
        return range(first, first + MEMBERS)

    def frame_of(unit):
        return 4 * plane + 2 * ((role + unit % 2) % 2) + core

    def rows_of(m):
        return pl.ds(pl.multiple_of(m * TOKENS, 64), TOKENS)

    def lanes_of(head):
        return pl.ds(pl.multiple_of(head * HD, HD), HD)

    loads = [
        pltpu.make_async_copy(k_hbm.at[0], k_in, load_sem.at[0]),
        pltpu.make_async_copy(q_hbm.at[0], q_in, load_sem.at[1]),
    ]
    for load in loads:
        load.start()

    barrier = pltpu.get_barrier_semaphore()

    def greet(device):
        pl.semaphore_signal(barrier, inc=1, device_id=device, device_id_type=MESH)

    first_idle = (NB + 11) * BLK
    for u in range(UNITS):
        for t in range(2):
            pairs[u, t, first_idle:, :] = jnp.zeros((KEYS - first_idle, HD), jnp.bfloat16)

    for i in range(1, 2 * MEMBERS):
        greet(place(i))
    greet((frame + 1 - 2 * core, member))
    expected = 2 * MEMBERS
    near = jnp.minimum(3 - plane, 1), jnp.minimum(plane, 1)
    far = (3 - plane) // 2, plane // 2
    far = jnp.minimum(far[0], 1), jnp.minimum(far[1], 1)
    across = core * near[0] + (1 - core) * near[1]
    side = 2 * core - 1
    meets = [
        (near[0], frame + 4), (near[1], frame - 4), (far[0], frame + 8), (far[1], frame - 8),
        (across, frame + 4 * side - side),
    ]
    for there, to in meets:
        expected = expected + there

        @pl.when(there > 0)
        def _():
            greet((to, member))

    def target_frame(f, segment):
        distance, direction, _, _ = SEGMENTS[segment]
        return f + distance if direction == 0 else f - distance

    def clipped(f):
        return jnp.clip(f, 0, FRAMES - 1)

    def role_of(f):
        return lax.rem(lax.div(f, 2), 2)

    def single_place(to):
        return to, flip(member, 4 * ((role_of(to) + role) % 2))

    for segment, (distance, direction, _, _) in enumerate(SEGMENTS):
        to = target_frame(frame, segment)
        there = reaches(frame, distance, 1 - direction)
        expected = expected + there

        @pl.when(there > 0)
        def _():
            greet(single_place(clipped(to)))

    pl.semaphore_wait(barrier, expected)

    def exchange(t, s, i):
        head, unit = head_at(s, i), unit_of(s, i)
        if t == 0:
            source, target = v_hbm.at[0, :, lanes_of(head)], pairs.at[unit, 1, rows_of(member)]
        elif t == 1:
            source, target = k_norm.at[head], pairs.at[unit, 0, rows_of(member)]
        else:
            source, target = q_norm.at[head], queries.at[unit, rows_of(member)]
        if i == 0:
            return pltpu.make_async_copy(source, target, own_sem.at[t, s])
        return pltpu.make_async_remote_copy(
            source, target, a2a_send.at[t], a2a_recv.at[t, unit],
            device_id=place(i), device_id_type=MESH,
        )

    def start_exchange(t, unit):
        for i in partners_of(unit):
            exchange(t, unit // 2, i).start()

    def wait_exchange(t, unit):
        rows = S
        if unit % 2 == 0:
            exchange(t, unit // 2, 0).wait()
            rows = S - TOKENS
        some = heads_out.at[0, pl.ds(0, rows)]
        pltpu.make_async_copy(some, some, a2a_recv.at[t, unit]).wait()

    def normalise(source, gain, target):
        scale = gain[...]

        def some_rows(i, carry):
            rows = pl.ds(pl.multiple_of(i * NORM_ROWS, NORM_ROWS), NORM_ROWS)
            wide = source[rows, :].astype(jnp.float32)
            meansq = jnp.mean(wide * wide, axis=-1, keepdims=True)
            normed = (wide * lax.rsqrt(meansq + EPSILON) * scale).astype(jnp.bfloat16)
            for head in range(HEADS):
                target[head, rows, :] = normed[:, head * HD : (head + 1) * HD]
            return carry

        lax.fori_loop(0, TOKENS // NORM_ROWS, some_rows, 0)

    def inside(f, segment, unit):
        distance, direction, _, _ = SEGMENTS[segment]
        there = reaches(f, distance, 1 - direction)
        if distance != 2 or unit == 4:
            return there, None
        here = 1 - role_of(f) if direction == 0 else role_of(f)
        return there * (1 - here), here

    def kept_copy(segment, unit):
        _, _, count, at = SEGMENTS[segment]
        to = clipped(target_frame(frame_of(unit), segment))
        start = pl.multiple_of(first_block(to, segment) * BLK, BLK)
        if unit == 4:
            device, its_unit = single_place(to), 4
        else:
            device = (4 * (to // 4) + 2 * role + to % 2, member)
            its_unit = 2 * (unit // 2) + (role_of(to) + role) % 2
        source, target = kept.at[unit, :, pl.ds(at * BLK, count * BLK)], pairs.at[its_unit, :, pl.ds(start, count * BLK)]
        return pltpu.make_async_remote_copy(
            source, target,
            kept_send.at[unit, segment], kept_recv.at[its_unit, segment],
            device_id=device, device_id_type=MESH,
        )

    def send_kept(unit):
        f = frame_of(unit)
        for t in range(2):
            stage[t] = pairs[unit, t, :S, :].reshape(NB, BLK, HD)
        for segment in ORDER:
            distance, direction, count, at = SEGMENTS[segment]
            there, here = inside(f, segment, unit)
            to = clipped(target_frame(f, segment))

            def chosen(i):
                keep = keeps[distance]
                return keep[i, direction, to] if count > 1 else keep[direction, i, to]

            @pl.when(there > 0)
            def _():
                for i in range(count):
                    block = chosen(i)
                    for t in range(2):
                        kept[unit, t, (at + i) * BLK : (at + i + 1) * BLK, :] = stage[t, block]
                kept_copy(segment, unit).start()

            if here is not None:
                start = first_block(to, segment)

                @pl.when(here > 0)
                def _():
                    for i in range(count):
                        block = chosen(i)
                        rows = pl.ds(pl.multiple_of((start + i) * BLK, BLK), BLK)
                        for t in range(2):
                            pairs[unit ^ 1, t, rows, :] = stage[t, block]

    def wait_kept(unit):
        f = frame_of(unit)
        for segment, (distance, direction, count, _) in enumerate(SEGMENTS):
            there = reaches(f, distance, direction)
            if distance == 2 and unit != 4:
                there = there * (1 - role_of(f) if direction == 0 else role_of(f))

            @pl.when(there > 0)
            def _():
                start = pl.multiple_of(first_block(f, segment) * BLK, BLK)
                target = pairs.at[unit, :, pl.ds(start, count * BLK)]
                pltpu.make_async_copy(target, target, kept_recv.at[unit, segment]).wait()

    def weigh(q, u, first, last, usable):
        scores = nt_dot(q, pairs[u, 0, first * BLK : last * BLK, :])
        parts = []
        for b in range(first, last):
            part = scores[:, (b - first) * BLK : (b - first + 1) * BLK]
            if b >= NB + 11:
                part = part + jnp.where(b < usable, 0.0, NEGATIVE)
            parts.append(part)
        peak = functools.reduce(jnp.maximum, parts)
        return parts, jnp.max(peak, axis=1, keepdims=True) * SCALE

    def gather(parts, above, u, first, last):
        weights = jnp.concatenate(
            [jnp.exp2(part * SCALE - above).astype(jnp.bfloat16) for part in parts], axis=1
        )
        wide = jnp.concatenate(
            [pairs[u, 1, first * BLK : last * BLK, :], jnp.ones(((last - first) * BLK, HD), jnp.bfloat16)], axis=1
        )
        product = jnp.dot(weights, wide, preferred_element_type=jnp.float32)
        return product[:, :HD], product[:, HD:]

    def tile_rows(i):
        return pl.ds(pl.multiple_of(i * TQ, TQ), TQ)

    def attend_own(u, n, i):
        rows = tile_rows(i)
        parts, peak = weigh(queries[u, rows, :], u, 0, NB, NB)
        above = jnp.broadcast_to(peak, (TQ, HD))
        running[n, 0, rows, :] = above
        running[n, 1, rows, :], running[n, 2, rows, :] = gather(parts, above, u, 0, NB)

    def attend_kept(u, n, i):
        rows = tile_rows(i)
        usable = first_block(frame_of(u), len(SEGMENTS)) + 1
        q = queries[u, rows, :]
        top, summed, total = running[n, 0, rows, :], running[n, 1, rows, :], running[n, 2, rows, :]
        for first, last in CHUNKS:
            parts, peak = weigh(q, u, first, last, usable)
            above = jnp.maximum(top, peak)
            fade = jnp.exp2(top - above)
            product, sums = gather(parts, above, u, first, last)
            summed = summed * fade + product
            total = total * fade + sums
            top = above
        heads_out[u, rows, :] = (summed / total).astype(jnp.bfloat16)

    def give_back(s, i):
        unit, lanes = unit_of(s, i), lanes_of(head_at(s, 0))
        source, target = heads_out.at[unit, rows_of(members[i % MEMBERS])], out_hbm.at[0, :, lanes]
        if i == 0:
            return pltpu.make_async_copy(source, target, own_sem.at[3, s])
        return pltpu.make_async_remote_copy(
            source, target, out_send.at[0], out_recv.at[0], device_id=place(i), device_id_type=MESH
        )

    def give(unit):
        for i in partners_of(unit):
            give_back(unit // 2, i).start()

    def take(*tensors):
        for t, unit in tensors:
            wait_exchange(t, unit)

    def give_rows(unit, first, last):
        s, other = unit // 2, unit % 2
        for m in range(first, last):
            j = flip(member, m)
            source = heads_out.at[unit, m * TOKENS : (m + 1) * TOKENS]
            target = out_hbm.at[0, :, lanes_of(head_at(s, 0))]

            def send():
                pltpu.make_async_remote_copy(
                    source, target, out_send.at[0], out_recv.at[0],
                    device_id=(4 * plane + 2 * roles[other] + core, m), device_id_type=MESH,
                ).start()

            if other:
                send()
                continue
            pl.when(j > 0)(send)

            @pl.when(j == 0)
            def _():
                pltpu.make_async_copy(source, target, own_sem.at[3, s]).start()

    start_exchange(0, 4)
    start_exchange(0, 1)
    loads[0].wait()
    normalise(k_in, k_gain, k_norm)
    start_exchange(1, 4)
    start_exchange(1, 1)
    loads[1].wait()
    normalise(q_in, q_gain, q_norm)
    start_exchange(2, 4)
    start_exchange(2, 1)
    for t in range(3):
        start_exchange(t, 0)
    for unit in (3, 2):
        for t in range(3):
            start_exchange(t, unit)
    take((0, 4), (1, 4))
    send_kept(4)

    own, others = 0, 1
    values_keys = lambda unit: take((0, unit), (1, unit))

    def before_own(unit):
        values_keys(unit)
        send_kept(unit)
        take((2, unit))

    def before_others(unit, done):
        give(done)
        wait_kept(unit)

    def serve(unit):
        values_keys(unit)
        send_kept(unit)

    def before_others_1():
        serve(3)
        wait_kept(1)

    def before_own_3():
        give(1)
        take((2, 3))

    def before_own_2():
        give(0)
        take((2, 2))

    phases = [
        (own, 4, 0, TILES, lambda: take((2, 4))),
        (own, 1, 0, TILES, lambda: before_own(1)),
        (own, 0, 0, TILES, lambda: before_own(0)),
        (others, 1, 0, TILES, before_others_1),
        (own, 3, 0, TILES, before_own_3),
        (others, 0, 0, 1, lambda: wait_kept(0)),
        (others, 0, 1, TILES, lambda: serve(2)),
        (own, 2, 0, TILES, before_own_2),
        (others, 4, 0, TILES, lambda: wait_kept(4)),
        (others, 3, 0, TILES, lambda: before_others(3, 4)),
        (others, 2, 0, 1, lambda: before_others(2, 3)),
        (others, 2, 1, TILES, lambda: give_rows(2, 0, 4)),
    ]

    def pick(n, column):
        return functools.reduce(lambda v, k: jnp.where(n == k, phases[k][column], v), range(len(phases)), 0)

    def phase(n, carry):
        kind, unit, first, last = (pick(n, column) for column in range(4))
        for k, (_, _, _, _, todo) in enumerate(phases):
            if todo is not None:
                pl.when(n == k)(todo)

        def own_tile(i, c):
            attend_own(unit, unit, i)
            return c

        def kept_tile(i, c):
            attend_kept(unit, unit, i)
            return c

        lax.fori_loop(first, jnp.where(kind == own, last, first), own_tile, 0)
        lax.fori_loop(first, jnp.where(kind == own, first, last), kept_tile, 0)
        return carry

    lax.fori_loop(0, len(phases), phase, 0)
    give_rows(2, 4, 8)

    for s in range(3):
        give_back(s, 0).wait()
    copies = k_norm.at[pl.ds(0, MEMBERS * UNITS - 3)]
    for semaphore in (a2a_send.at[0], a2a_send.at[1], a2a_send.at[2], out_send.at[0], out_recv.at[0]):
        pltpu.make_async_copy(copies, copies, semaphore).wait()
    for unit in range(UNITS):
        for segment in range(len(SEGMENTS)):
            @pl.when(inside(frame_of(unit), segment, unit)[0] > 0)
            def _():
                kept_copy(segment, unit).wait_send()


def on_device(q_in, k_in, v_in, q_gain, k_gain, keep_one, keep_two, keep_four, keep_eight):
    hbm = pl.BlockSpec(memory_space=pl.ANY)
    vmem = pl.BlockSpec(memory_space=pltpu.VMEM)
    smem = pl.BlockSpec(memory_space=pltpu.SMEM)
    bf16 = jnp.bfloat16
    dma = pltpu.SemaphoreType.DMA
    return pl.pallas_call(
        kernel,
        out_shape=pltpu.VMEM((1, TOKENS, WIDTH), bf16),
        in_specs=[hbm, hbm, hbm, vmem, vmem, smem, smem, smem, smem],
        out_specs=vmem,
        scratch_shapes=[
            pltpu.VMEM((TOKENS, WIDTH), bf16),
            pltpu.VMEM((TOKENS, WIDTH), bf16),
            pltpu.VMEM((HEADS, TOKENS, HD), bf16),
            pltpu.VMEM((HEADS, TOKENS, HD), bf16),
            pltpu.VMEM((UNITS, S, HD), bf16),
            pltpu.VMEM((UNITS, 2, KEYS, HD), bf16),
            pltpu.VMEM((2, NB, BLK, HD), bf16),
            pltpu.VMEM((UNITS, 2, KEPT * BLK, HD), bf16),
            pltpu.VMEM((UNITS, S, HD), bf16),
            pltpu.VMEM((UNITS, 3, S, HD), jnp.float32),
            dma((2,)),
            dma((4, 3)),
            dma((3,)),
            dma((3, UNITS)),
            dma((UNITS, len(SEGMENTS))),
            dma((UNITS, len(SEGMENTS))),
            dma((1,)),
            dma((1,)),
        ],
        compiler_params=pltpu.CompilerParams(
            collective_id=0, has_side_effects=True, vmem_limit_bytes=56 * 2**20
        ),
        cost_estimate=pl.CostEstimate(
            flops=4 * S * KEYS * PER * HD, bytes_accessed=8 * TOKENS * WIDTH, transcendentals=S * KEYS * PER
        ),
        name="attend",
    )(
        q_in, k_in, v_in, q_gain.reshape(1, WIDTH), k_gain.reshape(1, WIDTH),
        keep_one.transpose(2, 1, 0), keep_two.transpose(2, 1, 0),
        keep_four.transpose(1, 2, 0), keep_eight.transpose(1, 2, 0),
    )


def solution(mesh):
    return jax.shard_map(
        on_device,
        mesh=mesh,
        in_specs=(P("tm", "head", None),) * 3 + (P(),) * 6,
        out_specs=P("tm", "head", None),
        check_vma=False,
    )
```

```python
import functools
import math

import jax
import jax.numpy as jnp
from jax import lax
from jax.experimental import pallas as pl
from jax.experimental.pallas import tpu as pltpu
from jax.sharding import PartitionSpec as P

MESH = pl.DeviceIdType.MESH
HEADS = 40
HD = 128
BLK = 128
EPSILON = 1e-06
NEGATIVE = -1e30
LOG2E = math.log2(math.e)

FRAMES = 16
MEMBERS = 8
PER = HEADS // MEMBERS
TOKENS = 192
S = TOKENS * MEMBERS
NB = S // BLK
WIDTH = HEADS * HD
SEGMENTS = ((1, 0, 6, 0), (1, 1, 6, 6), (2, 0, 3, 12), (2, 1, 3, 15), (4, 0, 1, 18), (4, 1, 1, 19), (8, 0, 1, 20), (8, 1, 1, 20))
KEPT = 21
UNITS = 5
ORDER = (0, 1, 2, 3, 4, 5, 6, 7)
KEYS = (NB + KEPT) * BLK
TQ = 768
TILES = S // TQ
CHUNKS = ((NB, NB + 11), (NB + 11, NB + KEPT))
SCALE = LOG2E / math.sqrt(HD)
NORM_ROWS = 32


def nt_dot(a, b):
    return lax.dot_general(a, b, (((1,), (1,)), ((), ())), preferred_element_type=jnp.float32)


def reaches(frame, distance, direction):
    room = frame if direction == 0 else FRAMES - 1 - frame
    return jnp.minimum(lax.div(room, distance), 1)


def first_block(frame, segment):
    at = NB
    for distance, direction, count, _ in SEGMENTS[:segment]:
        if distance < 8:
            at = at + count * reaches(frame, distance, direction)
    return at


def kernel(
    q_hbm, k_hbm, v_hbm, q_gain, k_gain, keep_one, keep_two, keep_four, keep_eight,
    out_hbm,
    q_in, k_in, q_norm, k_norm, queries, pairs, stage, kept, heads_out, running,
    load_sem, own_sem, a2a_send, a2a_recv, kept_send, kept_recv, out_send, out_recv,
):
    frame = lax.axis_index("tm")
    member = lax.axis_index("head")
    plane, role, core = lax.div(frame, 4), lax.rem(lax.div(frame, 2), 2), lax.rem(frame, 2)
    keeps = {1: keep_one, 2: keep_two, 4: keep_four, 8: keep_eight}

    def bit(m, b):
        return (m // b) % 2 if isinstance(m, int) else lax.rem(lax.div(m, b), 2)

    def flip(m, bits):
        total = 0
        for b in (1, 2, 4):
            x = bit(m, b) + bit(bits, b)
            total = total + b * lax.rem(x, 2)
        return total

    roles = [lax.rem(role + other, 2) for other in range(2)]
    members = [flip(member, j) for j in range(MEMBERS)]

    def place(i):
        return 4 * plane + 2 * roles[i // MEMBERS] + core, members[i % MEMBERS]

    def head_at(s, i):
        its_role = roles[i // MEMBERS]
        group = flip(members[i % MEMBERS], 4 * its_role)
        return group * PER + (2 * its_role + s if s < 2 else 4)

    def unit_of(s, i):
        return 2 * s + i // MEMBERS if s < 2 else 4

    def partners_of(unit):
        first = MEMBERS * (unit % 2)
        return range(first, first + MEMBERS)

    def frame_of(unit):
        return 4 * plane + 2 * ((role + unit % 2) % 2) + core

    def rows_of(m):
        return pl.ds(pl.multiple_of(m * TOKENS, 64), TOKENS)

    def lanes_of(head):
        return pl.ds(pl.multiple_of(head * HD, HD), HD)

    loads = [
        pltpu.make_async_copy(k_hbm.at[0], k_in, load_sem.at[0]),
        pltpu.make_async_copy(q_hbm.at[0], q_in, load_sem.at[1]),
    ]
    for load in loads:
        load.start()

    barrier = pltpu.get_barrier_semaphore()

    def greet(device):
        pl.semaphore_signal(barrier, inc=1, device_id=device, device_id_type=MESH)

    first_idle = (NB + 11) * BLK
    for u in range(UNITS):
        for t in range(2):
            pairs[u, t, first_idle:, :] = jnp.zeros((KEYS - first_idle, HD), jnp.bfloat16)

    for i in range(1, 2 * MEMBERS):
        greet(place(i))
    greet((frame + 1 - 2 * core, member))
    expected = 2 * MEMBERS
    near = jnp.minimum(3 - plane, 1), jnp.minimum(plane, 1)
    far = (3 - plane) // 2, plane // 2
    far = jnp.minimum(far[0], 1), jnp.minimum(far[1], 1)
    across = core * near[0] + (1 - core) * near[1]
    side = 2 * core - 1
    meets = [
        (near[0], frame + 4), (near[1], frame - 4), (far[0], frame + 8), (far[1], frame - 8),
        (across, frame + 4 * side - side),
    ]
    for there, to in meets:
        expected = expected + there

        @pl.when(there > 0)
        def _():
            greet((to, member))

    def target_frame(f, segment):
        distance, direction, _, _ = SEGMENTS[segment]
        return f + distance if direction == 0 else f - distance

    def clipped(f):
        return jnp.clip(f, 0, FRAMES - 1)

    def role_of(f):
        return lax.rem(lax.div(f, 2), 2)

    def single_place(to):
        return to, flip(member, 4 * ((role_of(to) + role) % 2))

    for segment, (distance, direction, _, _) in enumerate(SEGMENTS):
        to = target_frame(frame, segment)
        there = reaches(frame, distance, 1 - direction)
        expected = expected + there

        @pl.when(there > 0)
        def _():
            greet(single_place(clipped(to)))

    pl.semaphore_wait(barrier, expected)

    def exchange(t, s, i):
        head, unit = head_at(s, i), unit_of(s, i)
        if t == 0:
            source, target = v_hbm.at[0, :, lanes_of(head)], pairs.at[unit, 1, rows_of(member)]
        elif t == 1:
            source, target = k_norm.at[head], pairs.at[unit, 0, rows_of(member)]
        else:
            source, target = q_norm.at[head], queries.at[unit, rows_of(member)]
        if i == 0:
            return pltpu.make_async_copy(source, target, own_sem.at[t, s])
        return pltpu.make_async_remote_copy(
            source, target, a2a_send.at[t], a2a_recv.at[t, unit],
            device_id=place(i), device_id_type=MESH,
        )

    def start_exchange(t, unit):
        for i in partners_of(unit):
            exchange(t, unit // 2, i).start()

    def wait_exchange(t, unit):
        rows = S
        if unit % 2 == 0:
            exchange(t, unit // 2, 0).wait()
            rows = S - TOKENS
        some = heads_out.at[0, pl.ds(0, rows)]
        pltpu.make_async_copy(some, some, a2a_recv.at[t, unit]).wait()

    def normalise(source, gain, target):
        scale = gain[...]

        def some_rows(i, carry):
            rows = pl.ds(pl.multiple_of(i * NORM_ROWS, NORM_ROWS), NORM_ROWS)
            wide = source[rows, :].astype(jnp.float32)
            meansq = jnp.mean(wide * wide, axis=-1, keepdims=True)
            normed = (wide * lax.rsqrt(meansq + EPSILON) * scale).astype(jnp.bfloat16)
            for head in range(HEADS):
                target[head, rows, :] = normed[:, head * HD : (head + 1) * HD]
            return carry

        lax.fori_loop(0, TOKENS // NORM_ROWS, some_rows, 0)

    def inside(f, segment, unit):
        distance, direction, _, _ = SEGMENTS[segment]
        there = reaches(f, distance, 1 - direction)
        if distance != 2 or unit == 4:
            return there, None
        here = 1 - role_of(f) if direction == 0 else role_of(f)
        return there * (1 - here), here

    def kept_copy(segment, unit):
        _, _, count, at = SEGMENTS[segment]
        to = clipped(target_frame(frame_of(unit), segment))
        start = pl.multiple_of(first_block(to, segment) * BLK, BLK)
        if unit == 4:
            device, its_unit = single_place(to), 4
        else:
            device = (4 * (to // 4) + 2 * role + to % 2, member)
            its_unit = 2 * (unit // 2) + (role_of(to) + role) % 2
        source, target = kept.at[unit, :, pl.ds(at * BLK, count * BLK)], pairs.at[its_unit, :, pl.ds(start, count * BLK)]
        return pltpu.make_async_remote_copy(
            source, target,
            kept_send.at[unit, segment], kept_recv.at[its_unit, segment],
            device_id=device, device_id_type=MESH,
        )

    def send_kept(unit):
        f = frame_of(unit)
        for t in range(2):
            stage[t] = pairs[unit, t, :S, :].reshape(NB, BLK, HD)
        for segment in ORDER:
            distance, direction, count, at = SEGMENTS[segment]
            there, here = inside(f, segment, unit)
            to = clipped(target_frame(f, segment))

            def chosen(i):
                keep = keeps[distance]
                return keep[i, direction, to] if count > 1 else keep[direction, i, to]

            @pl.when(there > 0)
            def _():
                for i in range(count):
                    block = chosen(i)
                    for t in range(2):
                        kept[unit, t, (at + i) * BLK : (at + i + 1) * BLK, :] = stage[t, block]
                kept_copy(segment, unit).start()

            if here is not None:
                start = first_block(to, segment)

                @pl.when(here > 0)
                def _():
                    for i in range(count):
                        block = chosen(i)
                        rows = pl.ds(pl.multiple_of((start + i) * BLK, BLK), BLK)
                        for t in range(2):
                            pairs[unit ^ 1, t, rows, :] = stage[t, block]

    def wait_kept(unit):
        f = frame_of(unit)
        for segment, (distance, direction, count, _) in enumerate(SEGMENTS):
            there = reaches(f, distance, direction)
            if distance == 2 and unit != 4:
                there = there * (1 - role_of(f) if direction == 0 else role_of(f))

            @pl.when(there > 0)
            def _():
                start = pl.multiple_of(first_block(f, segment) * BLK, BLK)
                target = pairs.at[unit, :, pl.ds(start, count * BLK)]
                pltpu.make_async_copy(target, target, kept_recv.at[unit, segment]).wait()

    def weigh(q, u, first, last, usable):
        scores = nt_dot(q, pairs[u, 0, first * BLK : last * BLK, :])
        parts = []
        for b in range(first, last):
            part = scores[:, (b - first) * BLK : (b - first + 1) * BLK]
            if b >= NB + 11:
                part = part + jnp.where(b < usable, 0.0, NEGATIVE)
            parts.append(part)
        peak = functools.reduce(jnp.maximum, parts)
        return parts, jnp.max(peak, axis=1, keepdims=True) * SCALE

    def gather(parts, above, u, first, last):
        weights = jnp.concatenate(
            [jnp.exp2(part * SCALE - above).astype(jnp.bfloat16) for part in parts], axis=1
        )
        wide = jnp.concatenate(
            [pairs[u, 1, first * BLK : last * BLK, :], jnp.ones(((last - first) * BLK, HD), jnp.bfloat16)], axis=1
        )
        product = jnp.dot(weights, wide, preferred_element_type=jnp.float32)
        return product[:, :HD], product[:, HD:]

    def tile_rows(i):
        return pl.ds(pl.multiple_of(i * TQ, TQ), TQ)

    def attend_own(u, n, i):
        rows = tile_rows(i)
        parts, peak = weigh(queries[u, rows, :], u, 0, NB, NB)
        above = jnp.broadcast_to(peak, (TQ, HD))
        running[n, 0, rows, :] = above
        running[n, 1, rows, :], running[n, 2, rows, :] = gather(parts, above, u, 0, NB)

    def attend_kept(u, n, i):
        rows = tile_rows(i)
        usable = first_block(frame_of(u), len(SEGMENTS)) + 1
        q = queries[u, rows, :]
        top, summed, total = running[n, 0, rows, :], running[n, 1, rows, :], running[n, 2, rows, :]
        for first, last in CHUNKS:
            parts, peak = weigh(q, u, first, last, usable)
            above = jnp.maximum(top, peak)
            fade = jnp.exp2(top - above)
            product, sums = gather(parts, above, u, first, last)
            summed = summed * fade + product
            total = total * fade + sums
            top = above
        heads_out[u, rows, :] = (summed / total).astype(jnp.bfloat16)

    def give_back(s, i):
        unit, lanes = unit_of(s, i), lanes_of(head_at(s, 0))
        source, target = heads_out.at[unit, rows_of(members[i % MEMBERS])], out_hbm.at[0, :, lanes]
        if i == 0:
            return pltpu.make_async_copy(source, target, own_sem.at[3, s])
        return pltpu.make_async_remote_copy(
            source, target, out_send.at[0], out_recv.at[0], device_id=place(i), device_id_type=MESH
        )

    def give(unit):
        for i in partners_of(unit):
            give_back(unit // 2, i).start()

    def take(*tensors):
        for t, unit in tensors:
            wait_exchange(t, unit)

    def give_rows(unit, first, last):
        s, other = unit // 2, unit % 2
        for m in range(first, last):
            j = flip(member, m)
            source = heads_out.at[unit, m * TOKENS : (m + 1) * TOKENS]
            target = out_hbm.at[0, :, lanes_of(head_at(s, 0))]

            def send():
                pltpu.make_async_remote_copy(
                    source, target, out_send.at[0], out_recv.at[0],
                    device_id=(4 * plane + 2 * roles[other] + core, m), device_id_type=MESH,
                ).start()

            if other:
                send()
                continue
            pl.when(j > 0)(send)

            @pl.when(j == 0)
            def _():
                pltpu.make_async_copy(source, target, own_sem.at[3, s]).start()

    start_exchange(0, 4)
    start_exchange(0, 1)
    loads[0].wait()
    normalise(k_in, k_gain, k_norm)
    start_exchange(1, 4)
    start_exchange(1, 1)
    loads[1].wait()
    normalise(q_in, q_gain, q_norm)
    start_exchange(2, 4)
    start_exchange(2, 1)
    for t in range(3):
        start_exchange(t, 0)
    for unit in (3, 2):
        for t in range(3):
            start_exchange(t, unit)
    take((0, 4), (1, 4))
    send_kept(4)

    own, others = 0, 1
    values_keys = lambda unit: take((0, unit), (1, unit))

    def before_own(unit):
        values_keys(unit)
        send_kept(unit)
        take((2, unit))

    def before_others(unit, done):
        give(done)
        wait_kept(unit)

    def midway():
        for unit in (2, 3):
            values_keys(unit)
            send_kept(unit)

    def before_own_2():
        give(0)
        take((2, 2))

    phases = [
        (own, 4, 0, TILES, lambda: take((2, 4))),
        (own, 1, 0, TILES, lambda: before_own(1)),
        (own, 0, 0, TILES, lambda: before_own(0)),
        (others, 1, 0, TILES, lambda: wait_kept(1)),
        (others, 0, 0, 1, lambda: before_others(0, 1)),
        (others, 0, 1, TILES, midway),
        (own, 2, 0, TILES, before_own_2),
        (own, 3, 0, TILES, lambda: take((2, 3))),
        (others, 4, 0, TILES, lambda: wait_kept(4)),
        (others, 3, 0, TILES, lambda: before_others(3, 4)),
        (others, 2, 0, 1, lambda: before_others(2, 3)),
        (others, 2, 1, TILES, lambda: give_rows(2, 0, 4)),
    ]

    def pick(n, column):
        return functools.reduce(lambda v, k: jnp.where(n == k, phases[k][column], v), range(len(phases)), 0)

    def phase(n, carry):
        kind, unit, first, last = (pick(n, column) for column in range(4))
        for k, (_, _, _, _, todo) in enumerate(phases):
            if todo is not None:
                pl.when(n == k)(todo)

        def own_tile(i, c):
            attend_own(unit, unit, i)
            return c

        def kept_tile(i, c):
            attend_kept(unit, unit, i)
            return c

        lax.fori_loop(first, jnp.where(kind == own, last, first), own_tile, 0)
        lax.fori_loop(first, jnp.where(kind == own, first, last), kept_tile, 0)
        return carry

    lax.fori_loop(0, len(phases), phase, 0)
    give_rows(2, 4, 8)

    for s in range(3):
        give_back(s, 0).wait()
    copies = k_norm.at[pl.ds(0, MEMBERS * UNITS - 3)]
    for semaphore in (a2a_send.at[0], a2a_send.at[1], a2a_send.at[2], out_send.at[0], out_recv.at[0]):
        pltpu.make_async_copy(copies, copies, semaphore).wait()
    for unit in range(UNITS):
        for segment in range(len(SEGMENTS)):
            @pl.when(inside(frame_of(unit), segment, unit)[0] > 0)
            def _():
                kept_copy(segment, unit).wait_send()


def on_device(q_in, k_in, v_in, q_gain, k_gain, keep_one, keep_two, keep_four, keep_eight):
    hbm = pl.BlockSpec(memory_space=pl.ANY)
    vmem = pl.BlockSpec(memory_space=pltpu.VMEM)
    smem = pl.BlockSpec(memory_space=pltpu.SMEM)
    bf16 = jnp.bfloat16
    dma = pltpu.SemaphoreType.DMA
    return pl.pallas_call(
        kernel,
        out_shape=pltpu.VMEM((1, TOKENS, WIDTH), bf16),
        in_specs=[hbm, hbm, hbm, vmem, vmem, smem, smem, smem, smem],
        out_specs=vmem,
        scratch_shapes=[
            pltpu.VMEM((TOKENS, WIDTH), bf16),
            pltpu.VMEM((TOKENS, WIDTH), bf16),
            pltpu.VMEM((HEADS, TOKENS, HD), bf16),
            pltpu.VMEM((HEADS, TOKENS, HD), bf16),
            pltpu.VMEM((UNITS, S, HD), bf16),
            pltpu.VMEM((UNITS, 2, KEYS, HD), bf16),
            pltpu.VMEM((2, NB, BLK, HD), bf16),
            pltpu.VMEM((UNITS, 2, KEPT * BLK, HD), bf16),
            pltpu.VMEM((UNITS, S, HD), bf16),
            pltpu.VMEM((UNITS, 3, S, HD), jnp.float32),
            dma((2,)),
            dma((4, 3)),
            dma((3,)),
            dma((3, UNITS)),
            dma((UNITS, len(SEGMENTS))),
            dma((UNITS, len(SEGMENTS))),
            dma((1,)),
            dma((1,)),
        ],
        compiler_params=pltpu.CompilerParams(
            collective_id=0, has_side_effects=True, vmem_limit_bytes=56 * 2**20
        ),
        cost_estimate=pl.CostEstimate(
            flops=4 * S * KEYS * PER * HD, bytes_accessed=8 * TOKENS * WIDTH, transcendentals=S * KEYS * PER
        ),
        name="attend",
    )(
        q_in, k_in, v_in, q_gain.reshape(1, WIDTH), k_gain.reshape(1, WIDTH),
        keep_one.transpose(2, 1, 0), keep_two.transpose(2, 1, 0),
        keep_four.transpose(1, 2, 0), keep_eight.transpose(1, 2, 0),
    )


def solution(mesh):
    return jax.shard_map(
        on_device,
        mesh=mesh,
        in_specs=(P("tm", "head", None),) * 3 + (P(),) * 6,
        out_specs=P("tm", "head", None),
        check_vma=False,
    )
```
